256 devices in a mesh: net: 4 (over z_hi, core), fsdp: 64 (over z_lo, x, y).
Axes of the slice: x: 4, y: 4, z: 8 (z_hi: 2, z_lo: 4; z = z_hi * 4 + z_lo), core: 2. Of those that a mesh axis runs over, the one named last changes fastest.
Arguments:
- noise_in: bfloat16 [8, 4096, 64], P(None, 'fsdp'), may hold values from -48 to 48
- renoise: bfloat16 [8, 4096, 64], P(None, 'fsdp'), may hold values from -6 to 6
- timesteps: int32 [8], replicated, may hold values from 20 to 979
- prompt_ids: int32 [8, 77], replicated, may hold values from 0 to 49407
- embed_w: bfloat16 [4, 64, 2432], P('net', None, 'fsdp'), may hold values from -0.75 to 0.75
- proj_w: bfloat16 [4, 2432, 2432], P('net', 'fsdp'), may hold values from -0.125 to 0.125
- final_w: bfloat16 [4, 2432, 64], P('net', 'fsdp'), may hold values from -0.125 to 0.125
- text_table: bfloat16 [49408, 64], P(('net', 'fsdp')), may hold values from -6 to 6
Outputs:
- sample_grad: float32 [8, 4096, 64], P(None, 'fsdp')
The draws below stay inside these ranges and needn't reach their ends.
All inputs are finite; a program needn't handle non-finite values. Where the reference program divides by a largest or mean magnitude, that divisor is 1e-20 or more.
Results may differ from the reference program's by a relative error of at most 0.0048.
Values may be sent and summed in bfloat16 or wider, within the bound.
No kernel may reach another device: no remote copies, remote signals or barrier semaphores. Data moves between devices by JAX's collectives and lax.ppermute only.
A program may use at most 128 MiB of HBM per device.

```python
import math
import jax
import jax.numpy as jnp
import numpy as np
from jax import lax

D = 2432
PATCH = 64
VOCAB = 49408
TXT = 77
PROMPTS = 8
IMG = 4096
GROUPS = 4


def draw_noise_in(key, part):
    key = jax.random.fold_in(key, 11)
    key_values, key_columns, key_start, key_end = jax.random.split(key, 4)
    position = jnp.arange(IMG, dtype=jnp.float32) / IMG
    col_scale = 1.0 + jax.random.uniform(key_columns, (PATCH,), jnp.float32)
    start_mean = jnp.clip(jax.random.normal(key_start, (PATCH,), jnp.float32), -3.0, 3.0)
    end_mean = jnp.clip(jax.random.normal(key_end, (PATCH,), jnp.float32), -3.0, 3.0)
    blend = (1.0 - position)[:, None] * start_mean[None, :] + position[:, None] * end_mean[None, :]
    values = jnp.clip(jax.random.normal(key_values, (PROMPTS, IMG, PATCH), jnp.float32), -6.0, 6.0) + 0.6 * blend[None, :, :]
    row_scale = 0.5 * jnp.exp(position * jnp.log(8.0))
    result = jnp.clip(values * row_scale[None, :, None] * col_scale[None, None, :], -47.0, 47.0)
    return result.astype(jnp.bfloat16)


def place_ends(array, key, low, largest):
    place = [jax.random.randint(jax.random.fold_in(key, axis), (), 0, length) for axis, length in enumerate(array.shape)]
    widest = array.shape.index(max(array.shape))
    beside = place[:widest] + [(place[widest] + 1) % array.shape[widest]] + place[widest + 1:]
    return array.at[tuple(place)].set(low).at[tuple(beside)].set(largest)


def steps_of(rng, dims, cuts, least, largest):
    factor_of = 1.0
    for dim, blocks in cuts:
        heights = jax.random.uniform(jax.random.fold_in(jax.random.fold_in(rng, 6), dim), (blocks,), jnp.float32, least / len(cuts), largest / len(cuts))
        factor_of = factor_of * jnp.repeat(jnp.exp(heights), dims[dim] // blocks).reshape((-1,) + (1,) * (len(dims) - 1 - dim))
    return factor_of


def cumulative_ranks(number_of, skew):
    weights = [(1 << 20) // math.isqrt(standing ** skew) + 1 for standing in range(1, number_of + 1)]
    deviation = 1 + sum(weights) // (1 << 30)
    return np.cumsum(np.array([max(1, weight // deviation) for weight in weights]))


def ranked(own_key, dims, count, lean):
    grid = cumulative_ranks(count, lean)
    pick = jax.random.randint(jax.random.fold_in(own_key, 1), dims, 0, int(grid[count - 1]))
    standing = jnp.searchsorted(jnp.asarray(grid, jnp.int32), pick, side="right")
    return jax.random.permutation(jax.random.fold_in(own_key, 2), count)[standing].astype(jnp.int32)


def bell_draw(own_key, dims, spread, limit, cuts=(), held_as=jnp.bfloat16):
    values = jax.random.normal(own_key, dims, jnp.float32) * spread
    if len(cuts) > 0:
        values = steps_of(own_key, dims, cuts, -0.22, 0.18) * values
    return jnp.clip(values, min=-limit, max=limit).astype(held_as)


def setup_inputs(seed: int = 0) -> dict:
    arg_keys = jax.random.split(jax.random.key(seed), 9)
    return {
        "noise_in": draw_noise_in(jax.random.fold_in(arg_keys[8], 71), 0),
        "renoise": bell_draw(arg_keys[1], (PROMPTS, IMG, PATCH), 1.0, 6.0, ((1, 64),)),
        "timesteps": place_ends(jax.random.randint(arg_keys[2], (PROMPTS,), 20, 980), jax.random.fold_in(arg_keys[2], 1), 20, 979).astype(jnp.int32),
        "prompt_ids": place_ends(ranked(arg_keys[3], (PROMPTS, TXT), VOCAB, 2), jax.random.fold_in(arg_keys[3], 3), 0, VOCAB - 1).astype(jnp.int32),
        "embed_w": bell_draw(arg_keys[4], (GROUPS, PATCH, D), PATCH ** -0.5, 0.75, ((0, 4), (2, 64))),
        "proj_w": bell_draw(arg_keys[5], (GROUPS, D, D), D ** -0.5, 0.125, ((0, 4), (1, 64))),
        "final_w": bell_draw(arg_keys[6], (GROUPS, D, PATCH), D ** -0.5, 0.125, ((0, 4), (1, 64))),
        "text_table": bell_draw(arg_keys[7], (VOCAB, PATCH), 1.0, 6.0, ((0, 256),)),
    }


epsilon = 1e-06

def forward_net(latent, embed_mat, proj_mat, final_mat):
    hidden = jnp.dot(latent, embed_mat, preferred_element_type=jnp.float32)
    active = jax.nn.gelu(hidden).astype(jnp.bfloat16)
    mixed_rows = hidden + jnp.dot(active, proj_mat, preferred_element_type=jnp.float32)
    factor = lax.rsqrt(lax.optimization_barrier(jnp.mean(mixed_rows * mixed_rows, axis=-1, keepdims=True)) + epsilon)
    normed = (mixed_rows * factor).astype(jnp.bfloat16)
    output = latent.astype(jnp.float32) + jnp.dot(normed, final_mat, preferred_element_type=jnp.float32)
    return (output, hidden, mixed_rows, factor)

def backward_net(back_rows, pulled_rows, hidden, mixed_rows, factor, embed_mat, proj_mat):
    unit_rows = mixed_rows * factor
    dmixed = factor * (back_rows - unit_rows * lax.optimization_barrier(jnp.mean(back_rows * unit_rows, axis=-1, keepdims=True)))
    dactive = lax.dot_general(dmixed.astype(jnp.bfloat16), proj_mat, (((1,), (1,)), ((), ())), preferred_element_type=jnp.float32)
    _, pullback = jax.vjp(jax.nn.gelu, hidden)
    dhidden = (dmixed + pullback(dactive)[0]).astype(jnp.bfloat16)
    return lax.dot_general(dhidden, embed_mat, (((1,), (1,)), ((), ())), preferred_element_type=jnp.float32) + pulled_rows

def reward_cotangent(pooled, text_mean):
    pooled_norm = jnp.sqrt(lax.optimization_barrier(jnp.sum(pooled * pooled, axis=-1, keepdims=True)) + epsilon)
    text_norm = jnp.sqrt(lax.optimization_barrier(jnp.sum(text_mean * text_mean, axis=-1, keepdims=True)) + epsilon)
    unit_pool = pooled / pooled_norm
    unit_text = text_mean / text_norm
    reward = lax.optimization_barrier(jnp.sum(unit_pool * unit_text, axis=-1, keepdims=True))
    return (unit_text - reward * unit_pool) / pooled_norm

def reference(noise_in, renoise, timesteps, prompt_ids, embed_w, proj_w, final_w, text_table):
    levels = timesteps.astype(jnp.float32) / 1000.0

    def one_prompt(prompt_items):
        latent, fresh_noise, noise_level, token_ids = prompt_items
        student = forward_net(latent, embed_w[0], proj_w[0], final_w[0])[0]
        sample = student.astype(jnp.bfloat16)
        sample_f = sample.astype(jnp.float32)
        noisy_rows = ((1.0 - noise_level) * sample_f + noise_level * fresh_noise.astype(jnp.float32)).astype(jnp.bfloat16)
        noisy_f = noisy_rows.astype(jnp.float32)
        real_pred = noisy_f - noise_level * forward_net(noisy_rows, embed_w[1], proj_w[1], final_w[1])[0]
        fake_pred = noisy_f - noise_level * forward_net(noisy_rows, embed_w[2], proj_w[2], final_w[2])[0]
        weight = 1.0 / (jnp.mean(jnp.abs(sample_f - real_pred)) + epsilon)
        judged, hidden, mixed_rows, factor = forward_net(sample, embed_w[3], proj_w[3], final_w[3])
        pooled = lax.optimization_barrier(jnp.mean(judged, axis=0, keepdims=True))
        text_mean = lax.optimization_barrier(jnp.mean(text_table[token_ids].astype(jnp.float32), axis=0, keepdims=True))
        cotangent = reward_cotangent(pooled, text_mean)
        back_vec = jnp.dot(cotangent, final_w[3].astype(jnp.float32).T, precision=lax.Precision.HIGHEST)
        reward_grad = backward_net(back_vec, cotangent, hidden, mixed_rows, factor, embed_w[3], proj_w[3])
        return weight * (fake_pred - real_pred) - reward_grad
    return lax.map(one_prompt, (noise_in, renoise, levels, prompt_ids))
```

```python
import jax
import jax.numpy as jnp
from jax import lax
from jax.sharding import Mesh, PartitionSpec as P

epsilon = 1e-06
NET = ("h", "c")
FSDP = ("z", "x", "y")


def shift(n, k):
    return [(i, (i + k) % n) for i in range(n)]


def gather_axis(piece, axis):
    size = lax.axis_size(axis)
    me = lax.axis_index(axis)
    moved = [piece] + [lax.ppermute(piece, axis, shift(size, k)) for k in range(1, size)]
    return me, moved


def place(me, moved):
    size = len(moved)
    out = jnp.zeros((size,) + moved[0].shape, moved[0].dtype)
    for k, piece in enumerate(moved):
        out = lax.dynamic_update_index_in_dim(out, piece, lax.rem(me - k + size, size), 0)
    return out.reshape((size * moved[0].shape[0],) + moved[0].shape[1:])


def gather_weights(slab):
    z = lax.axis_index("z")
    low = lax.rem(z, 2) == 0
    other = lax.ppermute(slab, "z", [(0, 1), (1, 0), (2, 3), (3, 2)])
    pair = jnp.concatenate([jnp.where(low, slab, other), jnp.where(low, other, slab)], 0)
    far = lax.ppermute(pair, "z", [(0, 2), (2, 0), (1, 3), (3, 1)])
    first = z < 2
    part_a, part_b = jnp.where(first, pair, far), jnp.where(first, far, pair)
    part_a, part_b = lax.optimization_barrier((part_a, part_b))
    (xi, moved_a), (yi, moved_b) = gather_axis(part_a, "x"), gather_axis(part_b, "y")
    moved_a, moved_b = lax.optimization_barrier((moved_a, moved_b))
    part_a, part_b = lax.optimization_barrier((place(xi, moved_a), place(yi, moved_b)))
    (yi, moved_a), (xi, moved_b) = gather_axis(part_a, "y"), gather_axis(part_b, "x")
    moved_a, moved_b = lax.optimization_barrier((moved_a, moved_b))
    return place(yi, moved_a), place(xi, moved_b)


def forward_net(latent, embed_k, embed_n, proj_k, final_n):
    hidden_k = lax.dot_general(
        latent, embed_k, (((1,), (1,)), ((), ())), preferred_element_type=jnp.float32
    )
    active = jax.nn.gelu(hidden_k).astype(jnp.bfloat16)
    hidden_n = lax.dot_general(
        latent, embed_n, (((1,), (1,)), ((), ())), preferred_element_type=jnp.float32
    )
    mixed_rows = hidden_n + jnp.dot(active, proj_k, preferred_element_type=jnp.float32)
    factor = lax.rsqrt(jnp.mean(mixed_rows * mixed_rows, axis=-1, keepdims=True) + epsilon)
    normed = (mixed_rows * factor).astype(jnp.bfloat16)
    output = latent.astype(jnp.float32) + jnp.dot(
        normed, final_n, preferred_element_type=jnp.float32
    )
    return (output, hidden_k, mixed_rows, factor)


def backward_net(back_rows, pulled_rows, hidden_k, mixed_rows, factor, embed_k, embed_n, proj_k):
    unit_rows = mixed_rows * factor
    dmixed = factor * (
        back_rows - unit_rows * jnp.mean(back_rows * unit_rows, axis=-1, keepdims=True)
    )
    rounded = dmixed.astype(jnp.bfloat16)
    dactive = lax.dot_general(
        rounded, proj_k, (((1,), (1,)), ((), ())), preferred_element_type=jnp.float32
    )
    _, pullback = jax.vjp(jax.nn.gelu, hidden_k)
    through = pullback(dactive)[0].astype(jnp.bfloat16)
    return (
        jnp.dot(through, embed_k, preferred_element_type=jnp.float32)
        + jnp.dot(rounded, embed_n, preferred_element_type=jnp.float32)
        + pulled_rows
    )


def reward_cotangent(pooled, text_mean):
    pooled_norm = jnp.sqrt(jnp.sum(pooled * pooled, axis=-1, keepdims=True) + epsilon)
    text_norm = jnp.sqrt(jnp.sum(text_mean * text_mean, axis=-1, keepdims=True) + epsilon)
    unit_pool = pooled / pooled_norm
    unit_text = text_mean / text_norm
    reward = jnp.sum(unit_pool * unit_text, axis=-1, keepdims=True)
    return (unit_text - reward * unit_pool) / pooled_norm


def sum_group(value):
    blocks = jnp.broadcast_to(value, (64,) + value.shape)
    return jnp.sum(lax.all_to_all(blocks, FSDP, 0, 0), axis=0)


def sum_nets(value):
    for_all = value
    for k in range(1, 4):
        for_all = for_all + lax.ppermute(value, NET, shift(4, k))
    return for_all


def on_device(noise_in, renoise, timesteps, prompt_ids, embed_w, proj_w, final_w, text_table):
    network = lax.axis_index(NET)
    prompts, local_rows, channels = noise_in.shape
    image_rows = local_rows * lax.axis_size(FSDP)
    shard, width = proj_w.shape[1], proj_w.shape[2]
    slab = jnp.concatenate([proj_w[0], embed_w[0].T, final_w[0]], axis=1)
    slab = jnp.pad(slab, ((0, 2), (0, 0)))
    part_a, part_b = gather_weights(slab)
    proj_k = jnp.concatenate([part_a[:, :width], part_b[:, :width]], 0)
    embed_k = jnp.concatenate(
        [part_a[:, width : width + channels], part_b[:, width : width + channels]], 0
    )
    tail_a = part_a[:, width:].reshape(4, 4, 2, shard + 2, 2 * channels)[:, :, :, :shard]
    tail_b = part_b[:, width:].reshape(4, 4, 2, shard + 2, 2 * channels)[:, :, :, :shard]
    tail_a = tail_a.transpose(2, 1, 0, 3, 4).reshape(width // 2, 2 * channels)
    tail_b = tail_b.transpose(2, 0, 1, 3, 4).reshape(width // 2, 2 * channels)
    tail = jnp.concatenate([tail_a, tail_b], 0)
    embed_n, final_n = tail[:, :channels], tail[:, channels:]

    table_rows = text_table.shape[0]
    first_row = lax.axis_index(NET + FSDP) * table_rows
    offsets = prompt_ids - first_row
    matches = offsets[:, :, None] == jnp.arange(table_rows, dtype=jnp.int32)[None, None, :]
    counts = jnp.sum(matches.astype(jnp.float32), axis=1).astype(jnp.bfloat16)
    text_part = (
        jnp.dot(counts, text_table, preferred_element_type=jnp.float32) / prompt_ids.shape[1]
    )
    text_part = sum_nets(text_part)

    flat_noise = noise_in.reshape(prompts * local_rows, channels)
    sample = forward_net(flat_noise, embed_k, embed_n, proj_k, final_n)[0].astype(jnp.bfloat16)
    sample = jnp.where(network == 0, sample, jnp.zeros_like(sample)).reshape(256, 128)
    for target in range(1, 4):
        sample = sample + lax.ppermute(sample, NET, [(0, target)])
    sample = sample.reshape(prompts * local_rows, channels)
    levels = (timesteps.astype(jnp.float32) / 1000.0)[:, None, None]
    sample_f = sample.astype(jnp.float32).reshape(prompts, local_rows, channels)
    noisy_rows = ((1.0 - levels) * sample_f + levels * renoise.astype(jnp.float32)).astype(
        jnp.bfloat16
    )
    source = jnp.where(network == 3, sample, noisy_rows.reshape(prompts * local_rows, channels))
    output, hidden_k, mixed_rows, factor = forward_net(
        source, embed_k, embed_n, proj_k, final_n
    )
    judged = output.reshape(prompts, local_rows, channels)
    predicted = noisy_rows.astype(jnp.float32) - levels * judged
    abs_part = jnp.sum(jnp.abs(sample_f - predicted), axis=(1, 2)) / (image_rows * channels)
    pool_part = jnp.sum(judged, axis=1) / image_rows
    sums = sum_group(
        jnp.concatenate(
            [pool_part, text_part, jnp.broadcast_to(abs_part[:, None], (prompts, 128))], 1
        )
    )
    term_sign = jnp.where(network == 1, -1.0, jnp.where(network == 2, 1.0, 0.0)).astype(jnp.float32)
    score_diff = sum_nets((term_sign * predicted).reshape(256, 128))
    pooled, text_mean, abs_total = sums[:, :64], sums[:, 64:128], sums[:, 128:]
    abs_total = sum_nets(jnp.where(network == 1, abs_total, 0.0))[:, 0]
    cotangent = reward_cotangent(pooled, text_mean)
    back_vec = jnp.dot(cotangent, final_n.astype(jnp.float32).T, precision=lax.Precision.HIGHEST)
    rows = prompts * local_rows
    back_rows = jnp.broadcast_to(back_vec[:, None, :], (prompts, local_rows, width)).reshape(
        rows, width
    )
    pulled_rows = jnp.broadcast_to(
        cotangent[:, None, :], (prompts, local_rows, channels)
    ).reshape(rows, channels)
    reward_grad = backward_net(
        back_rows, pulled_rows, hidden_k, mixed_rows, factor, embed_k, embed_n, proj_k
    )
    reward_grad = jnp.where(network == 3, reward_grad, 0.0).reshape(256, 128)
    reward_sum = sum_nets(reward_grad).reshape(prompts, local_rows, channels)
    score_diff = score_diff.reshape(prompts, local_rows, channels)
    weight = (1.0 / (abs_total + epsilon))[:, None, None]
    return weight * score_diff - reward_sum


def solution(mesh):
    cube = Mesh(mesh.devices.reshape(2, 2, 4, 4, 4), NET + FSDP)
    placed = (
        P(None, FSDP, None),
        P(None, FSDP, None),
        P(),
        P(),
        P(NET, None, FSDP),
        P(NET, FSDP, None),
        P(NET, FSDP, None),
        P(NET + FSDP, None),
    )
    return jax.shard_map(
        on_device, mesh=cube, in_specs=placed, out_specs=P(None, FSDP, None), check_vma=False
    )
```

```python
import jax
import jax.numpy as jnp
from jax import lax
from jax.experimental import pallas as pl
from jax.experimental.pallas import tpu as pltpu
from jax.sharding import Mesh, PartitionSpec as P

epsilon = 1e-06
NET = ("h", "c")
FSDP = ("z", "x", "y")
ROWS, CH, D, SHARD, PADDED = 512, 64, 2432, 38, 40
PIECE = 4 * PADDED
KDIM = 64 * PADDED
HALF = ROWS // 2
TILES = ((0, 512), (512, 512), (1024, 512), (1536, 512), (2048, 384))
VM = pl.BlockSpec(memory_space=pltpu.VMEM)
SM = pl.BlockSpec(memory_space=pltpu.SMEM)
NT = (((1,), (1,)), ((), ()))
f32, bf16 = jnp.float32, jnp.bfloat16


def call(body, outs, scratch=(), smem=0, ins=0):
    return pl.pallas_call(
        body,
        out_shape=[jax.ShapeDtypeStruct(s, t) for s, t in outs],
        in_specs=[SM] * smem + [VM] * ins,
        out_specs=[VM] * len(outs),
        scratch_shapes=list(scratch),
        compiler_params=pltpu.CompilerParams(vmem_limit_bytes=56 * 1024 * 1024),
    )


def mm(a, b):
    return jnp.dot(a, b, preferred_element_type=f32)


def mm_nt(a, b):
    return lax.dot_general(a, b, NT, preferred_element_type=f32)


def unpack(v):
    return jnp.concatenate([v[:, :CH], v[:, CH:]], axis=0)


def pack(v):
    return jnp.concatenate([v[:HALF], v[HALF:]], axis=1)


def prep_body(where_ref, *refs):
    pieces, (ek_ref, en_ref, tail_ref, ef_ref), (full, close) = refs[:16], refs[16:20], refs[20:]
    core, x, y = where_ref[0], where_ref[1], where_ref[2]
    for side in range(2):
        parity = core if side == 0 else 1 - core
        for part in range(2):
            z = 2 * part + parity
            for k in range(4):
                ref = pieces[side * 8 + part * 4 + k]
                tail = ref[:, D:].astype(f32)
                for i in range(4):
                    xs = i if part == 0 else lax.rem(x + 4 - k, 4)
                    ys = lax.rem(y + 4 - k, 4) if part == 0 else i
                    at = ((z * 4 + xs) * 4 + ys) * PADDED
                    full[pl.ds(pl.multiple_of(at, 8), PADDED), :] = tail[
                        i * PADDED : (i + 1) * PADDED
                    ]
                at_k = (side * 8 + part * 4 + k) * PIECE
                close[at_k : at_k + PIECE, :] = tail
    ek_ref[...] = close[...].T[:CH].astype(bf16)
    for d in range(64):
        close[d * SHARD : (d + 1) * SHARD, :] = full[d * PADDED : d * PADDED + SHARD, :]
    ordered = close[:D, :]
    tail_ref[...] = ordered.astype(bf16)
    flipped = ordered.T.astype(bf16)
    en_ref[...] = flipped[:CH]
    ef_ref[...] = mm(flipped[:CH], ordered[:, CH:].astype(bf16))


def prep(where, pieces):
    return call(
        prep_body,
        [((CH, KDIM), bf16), ((CH, D), bf16), ((D, 2 * CH), bf16), ((CH, CH), f32)],
        [pltpu.VMEM((KDIM, 2 * CH), f32), pltpu.VMEM((KDIM, 2 * CH), f32)],
        1,
        16,
    )(where, *pieces)


def forward(rows, ek_ref, en_ref, tail_ref, pieces, active, wide_mixed, normed):
    for at in range(0, KDIM, 512):
        active[:, at : at + 512] = jax.nn.gelu(mm(rows, ek_ref[:, at : at + 512])).astype(bf16)
    squares = jnp.zeros((ROWS, 128), f32)
    for at, wide in TILES:
        total = mm(rows, en_ref[:, at : at + wide])
        for side in range(2):
            block = jnp.concatenate(
                [ref[:, at : at + wide] for ref in pieces[side * 8 : side * 8 + 8]], axis=0
            )
            total += mm(active[:, side * 1280 : side * 1280 + 1280], block)
        wide_mixed[:, at : at + wide] = total
        for lane in range(0, wide, 128):
            squares += total[:, lane : lane + 128] * total[:, lane : lane + 128]
    mean = jnp.sum(squares, axis=1, keepdims=True) / D
    factor = lax.rsqrt(mean + epsilon)
    normed[...] = (wide_mixed[...] * factor).astype(bf16)
    return mm(normed[...], tail_ref[:, CH:]), factor


def student_body(rows_ref, ek_ref, en_ref, tail_ref, *refs):
    pieces, (out_ref, active, wide_mixed, normed) = refs[:16], refs[16:]
    rows = unpack(rows_ref[...])
    projected, _ = forward(rows, ek_ref, en_ref, tail_ref, pieces, active, wide_mixed, normed)
    out_ref[...] = pack((rows.astype(f32) + projected)).astype(bf16)


def student(rows, tables, pieces):
    return call(
        student_body,
        [((HALF, 128), bf16)],
        [
            pltpu.VMEM((ROWS, KDIM), bf16),
            pltpu.VMEM((ROWS, D), f32),
            pltpu.VMEM((ROWS, D), bf16),
        ],
        0,
        20,
    )(rows, *tables, *pieces)[0]


def second_body(sample_ref, renoise_ref, level_ref, text_ref, ek_ref, en_ref, tail_ref, *refs):
    pieces = refs[:16]
    rows_ref, pred_ref, sums_ref, proj_ref, factor_ref, normed, active, wide_mixed = refs[16:]
    level = level_ref[...]
    sample = sample_ref[...].astype(f32)
    packed = ((1.0 - level) * sample + level * renoise_ref[...].astype(f32)).astype(bf16)
    rows_ref[...] = packed
    rows = unpack(packed)
    projected, factor = forward(
        rows, ek_ref, en_ref, tail_ref, pieces, active, wide_mixed, normed
    )
    proj_ref[...] = projected
    factor_ref[...] = jnp.broadcast_to(factor, (ROWS, 128))
    judged = rows.astype(f32) + projected
    pred = packed.astype(f32) - level * pack(judged)
    pred_ref[...] = pred
    spread = jnp.abs(sample - pred)
    for p in range(4):
        part = jnp.sum(spread[p * 64 : p * 64 + 64], axis=0, keepdims=True)
        for q, cut in ((p, part[:, :CH]), (p + 4, part[:, CH:])):
            pool = jnp.sum(judged[q * 64 : q * 64 + 64], axis=0, keepdims=True)
            sums_ref[q : q + 1, :] = jnp.concatenate([pool, cut], axis=1)
    sums_ref[8:16, :] = text_ref[...]


def second(sample, renoise, level, text, tables, pieces):
    return call(
        second_body,
        [
            ((HALF, 128), bf16),
            ((HALF, 128), f32),
            ((16, 128), f32),
            ((ROWS, CH), f32),
            ((ROWS, 128), f32),
            ((ROWS, D), bf16),
        ],
        [pltpu.VMEM((ROWS, KDIM), bf16), pltpu.VMEM((ROWS, D), f32)],
        0,
        23,
    )(sample, renoise, level, text, *tables, *pieces)


def pf_body(tail_ref, *refs):
    pieces, out_ref = refs[:16], refs[16]
    final = tail_ref[:, CH:]
    for k, ref in enumerate(pieces):
        out_ref[k * PIECE : k * PIECE + PIECE, :] = mm(ref[:, :D], final)


def proj_final(tail, pieces):
    return call(pf_body, [((KDIM, CH), f32)], (), 0, 17)(tail, *pieces)[0]


def back_body(first, rows_ref, normed_ref, ek_ref, tail_ref, sum_ref, *refs):
    pieces, (out_ref, slope_ref) = refs[:4], refs[4:]
    rows = unpack(rows_ref[...])
    normed = normed_ref[...]
    hidden = mm(rows, ek_ref[...])
    s = 0.7978845608028654
    square = hidden * hidden
    th = jnp.tanh(s * hidden * (1.0 + 0.044715 * square))
    slope = 0.5 * (1.0 + th) + (0.5 * s) * hidden * (1.0 - th * th) * (1.0 + 0.134145 * square)
    slope_ref[...] = slope.astype(bf16)
    block = jnp.concatenate([ref[:, :D] for ref in pieces], axis=0)
    moved = (mm_nt(normed, block) * slope).astype(bf16)
    total = mm_nt(moved, ek_ref[...])
    if first:
        total += mm(normed, tail_ref[:, :CH])
    else:
        total += sum_ref[...]
    out_ref[...] = total


def back_step(first, rows, normed, ek, tail, total, pieces):
    return call(
        lambda *refs: back_body(first, *refs),
        [((ROWS, CH), f32), ((ROWS, 640), bf16)],
        (),
        0,
        9,
    )(rows, normed, ek, tail, total, *pieces)


def finish_body(sums_ref, shift_ref, ek_ref, pf_ref, ef_ref, proj_ref, factor_ref, total_ref, *refs):
    slopes, (cot_ref, out_ref) = refs[:4], refs[4:]
    high = lax.Precision.HIGHEST
    pooled = sums_ref[:8, :CH] / 4096.0
    text = sums_ref[8:16, :CH]
    pooled_norm = jnp.sqrt(jnp.sum(pooled * pooled, axis=-1, keepdims=True) + epsilon)
    text_norm = jnp.sqrt(jnp.sum(text * text, axis=-1, keepdims=True) + epsilon)
    unit_pool = pooled / pooled_norm
    unit_text = text / text_norm
    reward = jnp.sum(unit_pool * unit_text, axis=-1, keepdims=True)
    cot = (unit_text - reward * unit_pool) / pooled_norm
    carried = lax.dot_general(cot, pf_ref[...], NT, precision=high, preferred_element_type=f32)
    direct = lax.dot_general(cot, ef_ref[...], NT, precision=high, preferred_element_type=f32)

    def rows_of(v):
        return jnp.concatenate(
            [jnp.broadcast_to(v[p : p + 1], (64, v.shape[1])) for p in range(8)], axis=0
        )

    result = rows_of(direct)
    for j, ref in enumerate(slopes):
        scaled = ref[...].astype(f32) * rows_of(carried[:, j * 640 : j * 640 + 640])
        result += mm_nt(scaled.astype(bf16), ek_ref[:, j * 640 : j * 640 + 640])
    factor = factor_ref[:, :CH]
    cot_rows = rows_of(cot)
    along = jnp.sum(cot_rows * proj_ref[...], axis=1, keepdims=True) / D
    result = factor * (result - along * total_ref[...]) + cot_rows
    out_ref[...] = pack(result)
    cot_ref[...] = cot


def finish(sums, ek, pf, ef, projected, factor, total, slopes):
    return call(
        finish_body, [((8, CH), f32), ((HALF, 128), f32)], (), 0, 12
    )(sums, sums, ek, pf, ef, projected, factor, total, *slopes)[1]


def shift(n, k):
    return [(i, (i + k) % n) for i in range(n)]


Z1 = [(0, 1), (1, 0), (2, 3), (3, 2)]
Z2 = [(0, 2), (2, 0), (1, 3), (3, 1)]
CORE = [(0, 1), (1, 0)]


def gather_axis(piece, axis):
    return [piece] + [lax.ppermute(piece, axis, shift(4, k)) for k in range(1, 4)]


def place(me, moved):
    out = jnp.zeros((4,) + moved[0].shape, moved[0].dtype)
    for k, piece in enumerate(moved):
        out = lax.dynamic_update_index_in_dim(out, piece, lax.rem(me - k + 4, 4), 0)
    return out.reshape((4 * moved[0].shape[0],) + moved[0].shape[1:])


def gather_weights(slab):
    core, z, x, y = (lax.axis_index(a) for a in ("c", "z", "x", "y"))
    swapped = lax.ppermute(slab, ("c", "z"), [(4, 1), (1, 4), (6, 3), (3, 6)])
    mine = jnp.where(core == lax.rem(z, 2), slab, swapped)
    far = lax.ppermute(mine, "z", Z2)
    part_a, part_b = jnp.where(z < 2, mine, far), jnp.where(z < 2, far, mine)
    part_a, part_b = lax.optimization_barrier((part_a, part_b))
    moved_a, moved_b = gather_axis(part_a, "x"), gather_axis(part_b, "y")
    moved_a, moved_b = lax.optimization_barrier((moved_a, moved_b))
    part_a, part_b = lax.optimization_barrier((place(x, moved_a), place(y, moved_b)))
    pieces = gather_axis(part_a, "y") + gather_axis(part_b, "x")
    return pieces + [lax.ppermute(piece, "c", CORE) for piece in pieces]


def packed_rows(block):
    flat = block.reshape(ROWS, CH)
    return jnp.concatenate([flat[:HALF], flat[HALF:]], axis=1)


def on_device(noise_in, renoise, timesteps, prompt_ids, embed_w, proj_w, final_w, text_table):
    h, core, z, x, y = (lax.axis_index(a) for a in NET + FSDP)
    parity = lax.rem(z, 2)
    slab = jnp.concatenate([proj_w[0], embed_w[0].T, final_w[0]], axis=1)
    slab = jnp.pad(slab, ((0, PADDED - SHARD), (0, 0)))
    pieces = gather_weights(slab)

    both = jnp.concatenate([packed_rows(noise_in), packed_rows(renoise)], axis=0)
    other = lax.ppermute(both, "z", Z1)
    both = jnp.where(core == parity, both, other)
    noise, fresh = both[:HALF], both[HALF:]

    table_rows = text_table.shape[0]
    first_row = lax.axis_index(NET + FSDP) * table_rows
    offsets = prompt_ids - first_row
    matches = offsets[:, :, None] == jnp.arange(table_rows, dtype=jnp.int32)[None, None, :]
    counts = jnp.sum(matches.astype(f32), axis=1).astype(bf16)
    text = jnp.dot(counts, text_table, preferred_element_type=f32) / prompt_ids.shape[1]
    text = jnp.concatenate([text, jnp.zeros_like(text)], axis=1)
    text = text + lax.ppermute(text, "z", Z1)
    text = text + lax.ppermute(text, "h", CORE)

    judge = (h == 1) & (parity == 1)
    level = timesteps.astype(f32) / 1000.0
    level = jnp.where(judge, 0.0, level)
    level = jnp.broadcast_to(level[:, None, None], (8, 64, CH))
    level = packed_rows(level)

    where = jnp.stack([core, x, y]).astype(jnp.int32)
    ek, en, tail, ef = prep(where, pieces)
    tables = (ek, en, tail)
    sample = student(noise, tables, pieces)
    is_student = (h == 0) & (parity == 0)
    got = [
        lax.ppermute(sample, ("h", "z"), [(0, 5), (2, 7)]),
        lax.ppermute(sample, ("h", "z"), [(0, 4), (2, 6)]),
        lax.ppermute(sample, ("h", "z"), [(0, 1), (2, 3)]),
    ]
    sample = jnp.where(
        is_student, sample, jnp.where(h == 0, got[2], jnp.where(parity == 1, got[0], got[1]))
    )
    pf = proj_final(tail, pieces)
    rows, pred, sums, projected, factor, normed = second(sample, fresh, level, text, tables, pieces)

    real = lax.ppermute(pred, ("h", "z"), [(1, 5), (3, 7)])
    fake = lax.ppermute(pred, ("h", "z"), [(4, 5), (6, 7)])
    sums = sums + lax.ppermute(sums, "c", CORE)
    sums = sums + lax.ppermute(sums, "z", Z2)
    for axis in ("x", "y"):
        a, b, c, d = gather_axis(sums, axis)
        sums = (a + b) + (c + d)
    absolute = lax.ppermute(sums[:8], ("h", "z"), [(1, 5), (3, 7)])

    total = jnp.zeros((ROWS, CH), f32)
    slopes = []
    for j in range(4):
        total, slope = back_step(
            j == 0, rows, normed, ek[:, j * 640 : j * 640 + 640], tail, total,
            pieces[j * 4 : j * 4 + 4],
        )
        slopes.append(slope)
    reward = finish(sums, ek, pf, ef, projected, factor, total, slopes)
    weight = jnp.sum(absolute[:, CH:], axis=1) / (4096.0 * CH)
    weight = 1.0 / (weight + epsilon)
    weight = packed_rows(jnp.broadcast_to(weight[:, None, None], (8, 64, CH)))
    result = weight * (fake - real) - reward
    landed = 0.0
    for to_h in range(2):
        for to_c in range(2):
            pairs = [
                (9 + 4 * c + 2 * q, 8 * to_h + 4 * to_c + 2 * q + c)
                for c in range(2)
                for q in range(2)
            ]
            landed = landed + lax.ppermute(result, NET + ("z",), pairs)
    out = jnp.concatenate([landed[:, :CH], landed[:, CH:]], axis=0)
    return out.reshape(8, 64, CH)


def solution(mesh):
    cube = Mesh(mesh.devices.reshape(2, 2, 4, 4, 4), NET + FSDP)
    placed = (
        P(None, FSDP, None),
        P(None, FSDP, None),
        P(),
        P(),
        P(NET, None, FSDP),
        P(NET, FSDP, None),
        P(NET, FSDP, None),
        P(NET + FSDP, None),
    )
    return jax.shard_map(
        on_device, mesh=cube, in_specs=placed, out_specs=P(None, FSDP, None), check_vma=False
    )
```

```python
import jax
import jax.numpy as jnp
from jax import lax
from jax.experimental import pallas as pl
from jax.experimental.pallas import tpu as pltpu
from jax.sharding import Mesh, PartitionSpec as P

epsilon = 1e-06
NET = ("h", "c")
FSDP = ("z", "x", "y")
ROWS, CH, D, SHARD, PADDED = 512, 64, 2432, 38, 40
PIECE = 4 * PADDED
KDIM = 64 * PADDED
HALF = ROWS // 2
VM = pl.BlockSpec(memory_space=pltpu.VMEM)
SM = pl.BlockSpec(memory_space=pltpu.SMEM)
NT = (((1,), (1,)), ((), ()))
f32, bf16 = jnp.float32, jnp.bfloat16


def call(body, outs, scratch=(), smem=0, ins=0):
    return pl.pallas_call(
        body,
        out_shape=[jax.ShapeDtypeStruct(s, t) for s, t in outs],
        in_specs=[SM] * smem + [VM] * ins,
        out_specs=[VM] * len(outs),
        scratch_shapes=list(scratch),
        compiler_params=pltpu.CompilerParams(vmem_limit_bytes=28 * 1024 * 1024),
    )


def mm(a, b):
    return jnp.dot(a, b, preferred_element_type=f32)


def mm_nt(a, b):
    return lax.dot_general(a, b, NT, preferred_element_type=f32)


def unpack(v):
    return jnp.concatenate([v[:, :CH], v[:, CH:]], axis=0)


def pack(v):
    return jnp.concatenate([v[:HALF], v[HALF:]], axis=1)


def prep_body(where_ref, *refs):
    pieces, (full_ref, en_ref, fin_ref), wide = refs[:16], refs[16:19], refs[19]
    core, x, y = where_ref[0], where_ref[1], where_ref[2]
    for side in range(2):
        parity = core if side == 0 else 1 - core
        for part in range(2):
            z = 2 * part + parity
            for k in range(4):
                at_k = (side * 8 + part * 4 + k) * PIECE
                ref = pieces[side * 8 + part * 4 + k]

                def move(r, _, ref=ref, at_k=at_k):
                    at = pl.multiple_of(r * 16, 16)
                    full_ref[pl.ds(at_k + at, 16), :] = ref[pl.ds(at, 16), :]
                    return 0

                lax.fori_loop(0, PIECE // 16, move, 0)
                tail = ref[:, D:].astype(f32)
                for i in range(4):
                    xs = i if part == 0 else lax.rem(x + 4 - k, 4)
                    ys = lax.rem(y + 4 - k, 4) if part == 0 else i
                    at = ((z * 4 + xs) * 4 + ys) * PADDED
                    wide[pl.ds(pl.multiple_of(at, 8), PADDED), :] = tail[
                        i * PADDED : (i + 1) * PADDED
                    ]
    for d in range(64):
        wide[d * SHARD : (d + 1) * SHARD, :] = wide[d * PADDED : d * PADDED + SHARD, :]
    for at in range(0, D, 128):
        rows = wide[at : at + 128, :]
        en_ref[at : at + 128, :] = rows[:, :CH].astype(bf16)
        fin_ref[at : at + 128, :] = rows[:, CH:].astype(bf16)


def prep(where, pieces):
    return call(
        prep_body,
        [((KDIM, KDIM), bf16), ((D, CH), bf16), ((D, CH), bf16)],
        [pltpu.VMEM((KDIM, 2 * CH), f32)],
        1,
        16,
    )(where, *pieces)


def forward(rows, full_ref, en_ref, fin_ref, active, wide, normed, squares):
    def act(i, _):
        at = pl.multiple_of(i * 256, 256)
        hidden = mm_nt(rows, full_ref[pl.ds(at, 256), D : D + CH])
        active[:, pl.ds(at, 256)] = jax.nn.gelu(hidden).astype(bf16)
        return 0

    lax.fori_loop(0, KDIM // 256, act, 0)
    squares[...] = jnp.zeros((ROWS, 128), f32)

    def tile(at, size):
        total = mm(active[...], full_ref[:, pl.ds(at, size)])
        total += mm_nt(rows, en_ref[pl.ds(at, size), :])
        wide[:, pl.ds(at, size)] = total
        part = total[:, :128] * total[:, :128]
        if size > 128:
            part += total[:, 128:] * total[:, 128:]
        squares[...] += part

    def step(i, _):
        tile(pl.multiple_of(i * 256, 256), 256)
        return 0

    lax.fori_loop(0, 9, step, 0)
    tile(2304, 128)
    mean = jnp.sum(squares[...], axis=1, keepdims=True) / D
    factor = lax.rsqrt(mean + epsilon)
    squares[...] = jnp.broadcast_to(factor, (ROWS, 128))

    def scale(i, _):
        at = pl.multiple_of(i * 128, 128)
        normed[:, pl.ds(at, 128)] = (wide[:, pl.ds(at, 128)] * squares[...]).astype(bf16)
        return 0

    lax.fori_loop(0, D // 128, scale, 0)
    return mm(normed[...], fin_ref[...])


ACTIVE = pltpu.VMEM((ROWS, KDIM), bf16)
WIDE = pltpu.VMEM((ROWS, D), f32)
NORMED = pltpu.VMEM((ROWS, D), bf16)
SQUARES = pltpu.VMEM((ROWS, 128), f32)


def student_body(rows_ref, full_ref, en_ref, fin_ref, out_ref, active, wide, normed, squares):
    rows = unpack(rows_ref[...])
    projected = forward(rows, full_ref, en_ref, fin_ref, active, wide, normed, squares)
    out_ref[...] = pack((rows.astype(f32) + projected)).astype(bf16)


def student(rows, tables):
    return call(
        student_body, [((HALF, 128), bf16)], [ACTIVE, WIDE, NORMED, SQUARES], 0, 4
    )(rows, *tables)[0]


def second_body(sample_ref, renoise_ref, level_ref, text_ref, full_ref, en_ref, fin_ref, *refs):
    rows_ref, pred_ref, sums_ref, proj_ref, squares, normed, active, wide = refs
    level = level_ref[...]
    sample = sample_ref[...].astype(f32)
    packed = ((1.0 - level) * sample + level * renoise_ref[...].astype(f32)).astype(bf16)
    rows_ref[...] = packed
    rows = unpack(packed)
    projected = forward(rows, full_ref, en_ref, fin_ref, active, wide, normed, squares)
    proj_ref[...] = projected
    judged = rows.astype(f32) + projected
    pred = packed.astype(f32) - level * pack(judged)
    pred_ref[...] = pred
    spread = jnp.abs(sample - pred)
    for p in range(4):
        part = jnp.sum(spread[p * 64 : p * 64 + 64], axis=0, keepdims=True)
        for q, cut in ((p, part[:, :CH]), (p + 4, part[:, CH:])):
            pool = jnp.sum(judged[q * 64 : q * 64 + 64], axis=0, keepdims=True)
            sums_ref[q : q + 1, :] = jnp.concatenate([pool, cut], axis=1)
    sums_ref[8:16, :] = text_ref[...]


def second(sample, renoise, level, text, tables):
    return call(
        second_body,
        [
            ((HALF, 128), bf16),
            ((HALF, 128), f32),
            ((16, 128), f32),
            ((ROWS, CH), f32),
            ((ROWS, 128), f32),
            ((ROWS, D), bf16),
        ],
        [ACTIVE, WIDE],
        0,
        7,
    )(sample, renoise, level, text, *tables)


def pf_body(full_ref, en_ref, fin_ref, out_ref, ef_ref):
    def tile(i, _):
        at = pl.multiple_of(i * 256, 256)
        out_ref[pl.ds(at, 256), :] = mm(full_ref[pl.ds(at, 256), :D], fin_ref[...])
        return 0

    lax.fori_loop(0, KDIM // 256, tile, 0)
    ef_ref[...] = lax.dot_general(
        en_ref[...], fin_ref[...], (((0,), (0,)), ((), ())), preferred_element_type=f32
    )


def proj_final(tables):
    return call(pf_body, [((KDIM, CH), f32), ((CH, CH), f32)], (), 0, 3)(*tables)


CHUNKS = ((0, 3), (3, 3), (6, 2), (8, 2))


def back_body(base, tiles, rows_ref, normed_ref, full_ref, en_ref, sum_ref, out_ref, slope_ref):
    rows = unpack(rows_ref[...])
    if base == 0:
        out_ref[...] = mm(normed_ref[...], en_ref[...])
    else:
        out_ref[...] = sum_ref[...]

    def tile(i, _):
        at = pl.multiple_of(base * 256 + i * 256, 256)
        embed = full_ref[pl.ds(at, 256), D : D + CH]
        hidden = mm_nt(rows, embed)
        s = 0.7978845608028654
        square = hidden * hidden
        th = jnp.tanh(s * hidden * (1.0 + 0.044715 * square))
        slope = 0.5 * (1.0 + th) + (0.5 * s) * hidden * (1.0 - th * th) * (1.0 + 0.134145 * square)
        slope_ref[:, pl.ds(pl.multiple_of(i * 256, 256), 256)] = slope.astype(bf16)
        moved = mm_nt(normed_ref[...], full_ref[pl.ds(at, 256), :D]) * slope
        out_ref[...] += mm(moved.astype(bf16), embed)
        return 0

    lax.fori_loop(0, tiles, tile, 0)


def back_step(chunk, rows, normed, tables, total):
    base, tiles = chunk
    return call(
        lambda *refs: back_body(base, tiles, *refs),
        [((ROWS, CH), f32), ((ROWS, tiles * 256), bf16)],
        (),
        0,
        5,
    )(rows, normed, tables[0], tables[1], total)


def finish_body(sums_ref, full_ref, pf_ref, ef_ref, proj_ref, factor_ref, total_ref, *refs):
    slopes, out_ref, (carried, result) = refs[:4], refs[4], refs[5:]
    high = lax.Precision.HIGHEST
    pooled = sums_ref[:8, :CH] / 4096.0
    text = sums_ref[8:16, :CH]
    pooled_norm = jnp.sqrt(jnp.sum(pooled * pooled, axis=-1, keepdims=True) + epsilon)
    text_norm = jnp.sqrt(jnp.sum(text * text, axis=-1, keepdims=True) + epsilon)
    unit_pool = pooled / pooled_norm
    unit_text = text / text_norm
    reward = jnp.sum(unit_pool * unit_text, axis=-1, keepdims=True)
    cot = (unit_text - reward * unit_pool) / pooled_norm
    carried[...] = lax.dot_general(
        cot, pf_ref[...], NT, precision=high, preferred_element_type=f32
    )
    direct = lax.dot_general(cot, ef_ref[...], NT, precision=high, preferred_element_type=f32)

    def rows_of(v):
        return jnp.concatenate(
            [jnp.broadcast_to(v[p : p + 1], (64, v.shape[1])) for p in range(8)], axis=0
        )

    result[...] = rows_of(direct)
    for (base, tiles), ref in zip(CHUNKS, slopes):

        def tile(i, _, base=base, ref=ref):
            at = pl.multiple_of(base * 256 + i * 256, 256)
            local = pl.multiple_of(i * 256, 256)
            scaled = ref[:, pl.ds(local, 256)].astype(f32) * rows_of(carried[:, pl.ds(at, 256)])
            result[...] += mm(scaled.astype(bf16), full_ref[pl.ds(at, 256), D : D + CH])
            return 0

        lax.fori_loop(0, tiles, tile, 0)
    cot_rows = rows_of(cot)
    along = jnp.sum(cot_rows * proj_ref[...], axis=1, keepdims=True) / D
    out_ref[...] = pack(
        factor_ref[:, :CH] * (result[...] - along * total_ref[...]) + cot_rows
    )


def finish(sums, full, pf, ef, projected, factor, total, slopes):
    return call(
        finish_body,
        [((HALF, 128), f32)],
        [pltpu.VMEM((8, KDIM), f32), pltpu.VMEM((ROWS, CH), f32)],
        0,
        11,
    )(sums, full, pf, ef, projected, factor, total, *slopes)[0]


def shift(n, k):
    return [(i, (i + k) % n) for i in range(n)]


Z1 = [(0, 1), (1, 0), (2, 3), (3, 2)]
Z2 = [(0, 2), (2, 0), (1, 3), (3, 1)]
CORE = [(0, 1), (1, 0)]


def gather_axis(piece, axis):
    return [piece] + [lax.ppermute(piece, axis, shift(4, k)) for k in range(1, 4)]


def place(me, moved):
    out = jnp.zeros((4,) + moved[0].shape, moved[0].dtype)
    for k, piece in enumerate(moved):
        out = lax.dynamic_update_index_in_dim(out, piece, lax.rem(me - k + 4, 4), 0)
    return out.reshape((4 * moved[0].shape[0],) + moved[0].shape[1:])


def gather_weights(slab):
    core, z, x, y = (lax.axis_index(a) for a in ("c", "z", "x", "y"))
    swapped = lax.ppermute(slab, ("c", "z"), [(4, 1), (1, 4), (6, 3), (3, 6)])
    mine = jnp.where(core == lax.rem(z, 2), slab, swapped)
    far = lax.ppermute(mine, "z", Z2)
    part_a, part_b = jnp.where(z < 2, mine, far), jnp.where(z < 2, far, mine)
    part_a, part_b = lax.optimization_barrier((part_a, part_b))
    moved_a, moved_b = gather_axis(part_a, "x"), gather_axis(part_b, "y")
    moved_a, moved_b = lax.optimization_barrier((moved_a, moved_b))
    part_a, part_b = lax.optimization_barrier((place(x, moved_a), place(y, moved_b)))
    pieces = gather_axis(part_a, "y") + gather_axis(part_b, "x")
    near = [0, 4, 1, 3, 5, 7]
    ready = lax.optimization_barrier([pieces[i] for i in near])
    swaps = {i: lax.ppermute(v, "c", CORE) for i, v in zip(near, ready)}
    pieces = [ready[near.index(i)] if i in near else pieces[i] for i in range(8)]
    for i in (2, 6):
        swaps[i] = lax.ppermute(pieces[i], "c", CORE)
    return pieces + [swaps[i] for i in range(8)]


def packed_rows(block):
    flat = block.reshape(ROWS, CH)
    return jnp.concatenate([flat[:HALF], flat[HALF:]], axis=1)


def on_device(noise_in, renoise, timesteps, prompt_ids, embed_w, proj_w, final_w, text_table):
    h, core, z, x, y = (lax.axis_index(a) for a in NET + FSDP)
    parity = lax.rem(z, 2)
    slab = jnp.concatenate([proj_w[0], embed_w[0].T, final_w[0]], axis=1)
    slab = jnp.pad(slab, ((0, PADDED - SHARD), (0, 0)))
    pieces = gather_weights(slab)

    anchor, noise_in, renoise, prompt_ids = lax.optimization_barrier(
        (pieces[1], noise_in, renoise, prompt_ids)
    )
    pieces[1] = anchor
    both = jnp.concatenate([packed_rows(noise_in), packed_rows(renoise)], axis=0)
    other = lax.ppermute(both, "z", Z1)
    both = jnp.where(core == parity, both, other)
    noise, fresh = both[:HALF], both[HALF:]

    table_rows = text_table.shape[0]
    first_row = lax.axis_index(NET + FSDP) * table_rows
    offsets = prompt_ids - first_row
    matches = offsets[:, :, None] == jnp.arange(table_rows, dtype=jnp.int32)[None, None, :]
    counts = jnp.sum(matches.astype(f32), axis=1).astype(bf16)
    text = jnp.dot(counts, text_table, preferred_element_type=f32) / prompt_ids.shape[1]
    text = jnp.concatenate([text, jnp.zeros_like(text)], axis=1)
    text = text + lax.ppermute(text, "z", Z1)
    text = text + lax.ppermute(text, "h", CORE)

    judge = (h == 1) & (parity == 1)
    level = timesteps.astype(f32) / 1000.0
    level = jnp.where(judge, 0.0, level)
    level = jnp.broadcast_to(level[:, None, None], (8, 64, CH))
    level = packed_rows(level)

    where = jnp.stack([core, x, y]).astype(jnp.int32)
    tables = prep(where, pieces)
    sample = student(noise, tables)
    is_student = (h == 0) & (parity == 0)
    got = [
        lax.ppermute(sample, ("h", "z"), [(0, 5), (2, 7)]),
        lax.ppermute(sample, ("h", "z"), [(0, 4), (2, 6)]),
        lax.ppermute(sample, ("h", "z"), [(0, 1), (2, 3)]),
    ]
    sample, full, en, fin = lax.optimization_barrier((sample, *tables))
    pf, ef = proj_final((full, en, fin))
    got, sample, pf, text = lax.optimization_barrier((got, sample, pf, text))
    sample = jnp.where(
        is_student, sample, jnp.where(h == 0, got[2], jnp.where(parity == 1, got[0], got[1]))
    )
    rows, pred, sums, projected, factor, normed = second(sample, fresh, level, text, tables)

    real = lax.ppermute(pred, ("h", "z"), [(1, 5), (3, 7)])
    fake = lax.ppermute(pred, ("h", "z"), [(4, 5), (6, 7)])
    total = jnp.zeros((ROWS, CH), f32)
    slopes = []
    rounds = [[("c", CORE)], [("z", Z2)]] + [[(a, shift(4, k)) for k in (1, 2, 3)] for a in "xy"]
    for chunk, sends in zip(CHUNKS, rounds):
        sums, rows = lax.optimization_barrier((sums, rows))
        moved = [lax.ppermute(sums, axis, pairs) for axis, pairs in sends]
        total, slope = back_step(chunk, rows, normed, tables, total)
        total, moved = lax.optimization_barrier((total, moved))
        slopes.append(slope)
        sums = sum(moved, sums)
    absolute = lax.ppermute(sums[:8], ("h", "z"), [(1, 5), (3, 7)])
    reward = finish(sums, full, pf, ef, projected, factor, total, slopes)
    weight = jnp.sum(absolute[:, CH:], axis=1) / (4096.0 * CH)
    weight = 1.0 / (weight + epsilon)
    weight = packed_rows(jnp.broadcast_to(weight[:, None, None], (8, 64, CH)))
    result = weight * (fake - real) - reward
    landed = 0.0
    for to_h in range(2):
        for to_c in range(2):
            pairs = [
                (9 + 4 * c + 2 * q, 8 * to_h + 4 * to_c + 2 * q + c)
                for c in range(2)
                for q in range(2)
            ]
            landed = landed + lax.ppermute(result, NET + ("z",), pairs)
    out = jnp.concatenate([landed[:, :CH], landed[:, CH:]], axis=0)
    return out.reshape(8, 64, CH)


def solution(mesh):
    cube = Mesh(mesh.devices.reshape(2, 2, 4, 4, 4), NET + FSDP)
    placed = (
        P(None, FSDP, None),
        P(None, FSDP, None),
        P(),
        P(),
        P(NET, None, FSDP),
        P(NET, FSDP, None),
        P(NET, FSDP, None),
        P(NET + FSDP, None),
    )
    return jax.shard_map(
        on_device, mesh=cube, in_specs=placed, out_specs=P(None, FSDP, None), check_vma=False
    )
```

```python
import jax
import jax.numpy as jnp
from jax import lax
from jax.experimental import pallas as pl
from jax.experimental.pallas import tpu as pltpu
from jax.sharding import Mesh, PartitionSpec as P

epsilon = 1e-06
NET = ("h", "c")
FSDP = ("z", "x", "y")
ROWS, CH, D, SHARD, PADDED = 512, 64, 2432, 38, 40
PIECE = 4 * PADDED
KDIM = 64 * PADDED
CHUNK = KDIM // 4
SLOTS = ((0, 0, 160), (1, 0, 160), (2, 0, 80), (2, 80, 80), (3, 0, 160))
HALF = ROWS // 2
VM = pl.BlockSpec(memory_space=pltpu.VMEM)
SM = pl.BlockSpec(memory_space=pltpu.SMEM)
NT = (((1,), (1,)), ((), ()))
f32, bf16 = jnp.float32, jnp.bfloat16


def call(body, outs, scratch=(), smem=0, ins=0):
    return pl.pallas_call(
        body,
        out_shape=[jax.ShapeDtypeStruct(s, t) for s, t in outs],
        in_specs=[SM] * smem + [VM] * ins,
        out_specs=[VM] * len(outs),
        scratch_shapes=list(scratch),
        compiler_params=pltpu.CompilerParams(vmem_limit_bytes=20 * 1024 * 1024),
    )


def mm(a, b):
    return jnp.dot(a, b, preferred_element_type=f32)


def mm_nt(a, b):
    return lax.dot_general(a, b, NT, preferred_element_type=f32)


def unpack(v):
    return jnp.concatenate([v[:, :CH], v[:, CH:]], axis=0)


def pack(v):
    return jnp.concatenate([v[:HALF], v[HALF:]], axis=1)


def place_tail(part, k, row0, tail, wide, z, x, y):
    for i in range(tail.shape[0] // PADDED):
        inner = row0 // PADDED + i
        xs = inner if part == 0 else lax.rem(x + 4 - k, 4)
        ys = lax.rem(y + 4 - k, 4) if part == 0 else inner
        at = ((z * 4 + xs) * 4 + ys) * PADDED
        wide[pl.ds(pl.multiple_of(at, 8), PADDED), :] = tail[i * PADDED : (i + 1) * PADDED]


def prep_body(where_ref, *refs):
    pieces, (close_ref, en_ref, fin_ref), wide = refs[:20], refs[20:23], refs[23]
    core, x, y = where_ref[0], where_ref[1], where_ref[2]
    at_k = 0
    for side in range(2):
        parity = core if side == 0 else 1 - core
        for part in range(2):
            z = 2 * part + parity
            for slot, (k, row0, size) in enumerate(SLOTS):
                tail = pieces[side * 10 + part * 5 + slot][:, D:]
                close_ref[at_k : at_k + size, :] = tail[:, :CH]
                place_tail(part, k, row0, tail.astype(f32), wide, z, x, y)
                at_k += size
    for d in range(64):
        wide[d * SHARD : (d + 1) * SHARD, :] = wide[d * PADDED : d * PADDED + SHARD, :]

    def cut(i, _):
        at = pl.multiple_of(i * 128, 128)
        rows = wide[pl.ds(at, 128), :]
        en_ref[pl.ds(at, 128), :] = rows[:, :CH].astype(bf16)
        fin_ref[pl.ds(at, 128), :] = rows[:, CH:].astype(bf16)
        return 0

    lax.fori_loop(0, D // 128, cut, 0)


def prep(where, pieces):
    return call(
        prep_body,
        [((KDIM, CH), bf16), ((D, CH), bf16), ((D, CH), bf16)],
        [pltpu.VMEM((KDIM, 2 * CH), f32)],
        1,
        20,
    )(where, *pieces)


def forward(rows, close_ref, en_ref, fin_ref, pieces, active, wide, normed, squares):
    def act(i, _):
        at = pl.multiple_of(i * 256, 256)
        hidden = mm_nt(rows, close_ref[pl.ds(at, 256), :])
        active[:, pl.ds(at, 256)] = jax.nn.gelu(hidden).astype(bf16)
        return 0

    lax.fori_loop(0, KDIM // 256, act, 0)
    squares[...] = jnp.zeros((ROWS, 128), f32)

    def tile(at, size):
        block = jnp.concatenate([ref[:, pl.ds(at, size)] for ref in pieces], axis=0)
        for r in range(0, ROWS, HALF):
            total = mm(active[r : r + HALF, :], block)
            total += mm_nt(rows[r : r + HALF], en_ref[pl.ds(at, size), :])
            wide[r : r + HALF, pl.ds(at, size)] = total
            part = total[:, :128] * total[:, :128]
            for lane in range(128, size, 128):
                part += total[:, lane : lane + 128] * total[:, lane : lane + 128]
            squares[r : r + HALF] += part

    def step(i, _):
        tile(pl.multiple_of(i * 768, 256), 768)
        return 0

    lax.fori_loop(0, 3, step, 0)
    tile(2304, 128)
    mean = jnp.sum(squares[...], axis=1, keepdims=True) / D
    factor = lax.rsqrt(mean + epsilon)
    squares[...] = jnp.broadcast_to(factor, (ROWS, 128))

    def scale(i, _):
        at = pl.multiple_of(i * 128, 128)
        normed[:, pl.ds(at, 128)] = (wide[:, pl.ds(at, 128)] * squares[...]).astype(bf16)
        return 0

    lax.fori_loop(0, D // 128, scale, 0)
    return mm(normed[...], fin_ref[...])


ACTIVE = pltpu.VMEM((ROWS, KDIM), bf16)
WIDE = pltpu.VMEM((ROWS, D), f32)
NORMED = pltpu.VMEM((ROWS, D), bf16)
SQUARES = pltpu.VMEM((ROWS, 128), f32)


def student_body(rows_ref, close_ref, en_ref, fin_ref, *refs):
    pieces, (out_ref, active, wide, normed, squares) = refs[:20], refs[20:]
    rows = unpack(rows_ref[...])
    projected = forward(
        rows, close_ref, en_ref, fin_ref, pieces, active, wide, normed, squares
    )
    out_ref[...] = pack((rows.astype(f32) + projected)).astype(bf16)


def student(rows, tables, pieces):
    return call(
        student_body, [((HALF, 128), bf16)], [ACTIVE, WIDE, NORMED, SQUARES], 0, 24
    )(rows, *tables, *pieces)[0]


def second_body(sample_ref, renoise_ref, level_ref, text_ref, close_ref, en_ref, fin_ref, *refs):
    pieces = refs[:20]
    rows_ref, pred_ref, sums_ref, proj_ref, squares, normed, active, wide = refs[20:]
    level = level_ref[...]
    sample = sample_ref[...].astype(f32)
    packed = ((1.0 - level) * sample + level * renoise_ref[...].astype(f32)).astype(bf16)
    rows_ref[...] = packed
    rows = unpack(packed)
    projected = forward(
        rows, close_ref, en_ref, fin_ref, pieces, active, wide, normed, squares
    )
    proj_ref[...] = projected
    judged = rows.astype(f32) + projected
    pred = packed.astype(f32) - level * pack(judged)
    pred_ref[...] = pred
    spread = jnp.abs(sample - pred)
    for p in range(4):
        part = jnp.sum(spread[p * 64 : p * 64 + 64], axis=0, keepdims=True)
        for q, cut in ((p, part[:, :CH]), (p + 4, part[:, CH:])):
            pool = jnp.sum(judged[q * 64 : q * 64 + 64], axis=0, keepdims=True)
            sums_ref[q : q + 1, :] = jnp.concatenate([pool, cut], axis=1)
    sums_ref[8:16, :] = text_ref[...]


def second(sample, renoise, level, text, tables, pieces):
    return call(
        second_body,
        [
            ((HALF, 128), bf16),
            ((HALF, 128), f32),
            ((16, 128), f32),
            ((ROWS, CH), f32),
            ((ROWS, 128), f32),
            ((ROWS, D), bf16),
        ],
        [ACTIVE, WIDE],
        0,
        27,
    )(sample, renoise, level, text, *tables, *pieces)


def back_body(first, rows_ref, normed_ref, close_ref, en_ref, fin_ref, sum_ref, *refs):
    pieces, (out_ref, slope_ref, pf_ref), rest = refs[:5], refs[5:8], refs[8:]
    rows = rows_ref[...]
    if first:
        out_ref[...] = mm(normed_ref[...], en_ref[...])
        rest[0][...] = lax.dot_general(
            en_ref[...], fin_ref[...], (((0,), (0,)), ((), ())), preferred_element_type=f32
        )
    else:
        out_ref[...] = sum_ref[...]
    embed = close_ref[...]
    at = 0
    for ref in pieces:
        pf_ref[at : at + ref.shape[0], :] = mm(ref[:, :D], fin_ref[...])
        at += ref.shape[0]
    s = 0.7978845608028654
    for half in range(2):
        r = half * HALF
        hidden = mm_nt(rows[:, half * CH : half * CH + CH], embed)
        square = hidden * hidden
        th = jnp.tanh(s * hidden * (1.0 + 0.044715 * square))
        slope = 0.5 * (1.0 + th) + (0.5 * s) * hidden * (1.0 - th * th) * (1.0 + 0.134145 * square)
        slope_ref[r : r + HALF, :] = slope.astype(bf16)
        block = jnp.concatenate([ref[:, :D] for ref in pieces], axis=0)
        moved = mm_nt(normed_ref[r : r + HALF, :], block) * slope
        out_ref[r : r + HALF, :] += mm(moved.astype(bf16), embed)


def back_step(j, rows, normed, tables, total, pieces):
    close, en, fin = tables
    outs = [((ROWS, CH), f32), ((ROWS, CHUNK), bf16), ((CHUNK, CH), f32)]
    if j == 0:
        outs.append(((CH, CH), f32))
    return call(lambda *refs: back_body(j == 0, *refs), outs, (), 0, 11)(
        rows, normed, close[j * CHUNK : (j + 1) * CHUNK], en, fin, total, *pieces
    )


def finish_body(sums_ref, close_ref, ef_ref, proj_ref, factor_ref, total_ref, *refs):
    slopes, pfs, out_ref, result = refs[:4], refs[4:8], refs[8], refs[9]
    high = lax.Precision.HIGHEST
    pooled = sums_ref[:8, :CH] / 4096.0
    text = sums_ref[8:16, :CH]
    pooled_norm = jnp.sqrt(jnp.sum(pooled * pooled, axis=-1, keepdims=True) + epsilon)
    text_norm = jnp.sqrt(jnp.sum(text * text, axis=-1, keepdims=True) + epsilon)
    unit_pool = pooled / pooled_norm
    unit_text = text / text_norm
    reward = jnp.sum(unit_pool * unit_text, axis=-1, keepdims=True)
    cot = (unit_text - reward * unit_pool) / pooled_norm
    direct = lax.dot_general(cot, ef_ref[...], NT, precision=high, preferred_element_type=f32)

    def rows_of(v):
        return jnp.concatenate(
            [jnp.broadcast_to(v[p : p + 1], (64, v.shape[1])) for p in range(8)], axis=0
        )

    result[...] = rows_of(direct)
    for j, (slope, pf) in enumerate(zip(slopes, pfs)):
        carried = lax.dot_general(cot, pf[...], NT, precision=high, preferred_element_type=f32)
        scaled = slope[...].astype(f32) * rows_of(carried)
        result[...] += mm(scaled.astype(bf16), close_ref[j * CHUNK : (j + 1) * CHUNK, :])
    cot_rows = rows_of(cot)
    along = jnp.sum(cot_rows * proj_ref[...], axis=1, keepdims=True) / D
    out_ref[...] = pack(
        factor_ref[:, :CH] * (result[...] - along * total_ref[...]) + cot_rows
    )


def finish(sums, close, ef, projected, factor, total, slopes, pfs):
    return call(
        finish_body, [((HALF, 128), f32)], [pltpu.VMEM((ROWS, CH), f32)], 0, 14
    )(sums, close, ef, projected, factor, total, *slopes, *pfs)[0]


def shift(n, k):
    return [(i, (i + k) % n) for i in range(n)]


Z1 = [(0, 1), (1, 0), (2, 3), (3, 2)]
Z2 = [(0, 2), (2, 0), (1, 3), (3, 1)]
CORE = [(0, 1), (1, 0)]


def gather_axis(piece, axis):
    return [piece] + [lax.ppermute(piece, axis, shift(4, k)) for k in range(1, 4)]


def place(me, moved):
    out = jnp.zeros((4,) + moved[0].shape, moved[0].dtype)
    for k, piece in enumerate(moved):
        out = lax.dynamic_update_index_in_dim(out, piece, lax.rem(me - k + 4, 4), 0)
    return out.reshape((4 * moved[0].shape[0],) + moved[0].shape[1:])


def ring_step(to_right, to_left, axis):
    return lax.ppermute(to_right, axis, shift(4, 1)), lax.ppermute(to_left, axis, shift(4, 3))


def gather_weights(slab, exchange):
    core, z, x, y = (lax.axis_index(a) for a in ("c", "z", "x", "y"))
    swapped = lax.ppermute(slab, ("c", "z"), [(4, 1), (1, 4), (6, 3), (3, 6)])
    mine = jnp.where(core == lax.rem(z, 2), slab, swapped)
    far = lax.ppermute(mine, "z", Z2)
    part_a, part_b = jnp.where(z < 2, mine, far), jnp.where(z < 2, far, mine)
    part_a, part_b = lax.optimization_barrier((part_a, part_b))
    moved_a, moved_b = gather_axis(part_a, "x"), gather_axis(part_b, "y")
    moved_a, moved_b = lax.optimization_barrier((moved_a, moved_b))
    part_a, part_b = lax.optimization_barrier((place(x, moved_a), place(y, moved_b)))
    right_a, left_a = ring_step(part_a, part_a, "y")
    right_b, left_b = ring_step(part_b, part_b, "x")
    extra = exchange(part_a)
    right_a, left_a, right_b, left_b, extra = lax.optimization_barrier(
        (right_a, left_a, right_b, left_b, extra)
    )
    mid_a = ring_step(right_a[:80], left_a[80:], "y")
    mid_b = ring_step(right_b[:80], left_b[80:], "x")
    near = [part_a, right_a, left_a, part_b, right_b, left_b]
    far = [lax.ppermute(v, "c", CORE) for v in near]
    extra = extra[:-1] + (extra[-1] + lax.ppermute(extra[-1], "h", CORE),)
    mids, extra = lax.optimization_barrier(([*mid_a, *mid_b], extra))
    far_mids = [lax.ppermute(v, "c", CORE) for v in mids]

    def order(n, m):
        return [n[0], n[1], m[0], m[1], n[2], n[3], n[4], m[2], m[3], n[5]]

    return order(near, mids) + order(far, far_mids), extra


def packed_rows(block):
    flat = block.reshape(ROWS, CH)
    return jnp.concatenate([flat[:HALF], flat[HALF:]], axis=1)


def on_device(noise_in, renoise, timesteps, prompt_ids, embed_w, proj_w, final_w, text_table):
    h, core, z, x, y = (lax.axis_index(a) for a in NET + FSDP)
    parity = lax.rem(z, 2)
    slab = jnp.concatenate([proj_w[0], embed_w[0].T, final_w[0]], axis=1)
    slab = jnp.pad(slab, ((0, PADDED - SHARD), (0, 0)))

    def exchange(anchor):
        _, first, second_in, ids = lax.optimization_barrier(
            (anchor, noise_in, renoise, prompt_ids)
        )
        both = jnp.concatenate([packed_rows(first), packed_rows(second_in)], axis=0)
        other = lax.ppermute(both, "z", Z1)
        table_rows = text_table.shape[0]
        first_row = lax.axis_index(NET + FSDP) * table_rows
        offsets = ids - first_row
        matches = offsets[:, :, None] == jnp.arange(table_rows, dtype=jnp.int32)[None, None, :]
        counts = jnp.sum(matches.astype(f32), axis=1).astype(bf16)
        text = jnp.dot(counts, text_table, preferred_element_type=f32) / ids.shape[1]
        text = jnp.concatenate([text, jnp.zeros_like(text)], axis=1)
        text = text + lax.ppermute(text, "z", Z1)
        return jnp.where(core == parity, both, other), text

    pieces, (both, text) = gather_weights(slab, exchange)
    noise, fresh = both[:HALF], both[HALF:]
    judge = (h == 1) & (parity == 1)
    level = timesteps.astype(f32) / 1000.0
    level = jnp.where(judge, 0.0, level)
    level = jnp.broadcast_to(level[:, None, None], (8, 64, CH))
    level = packed_rows(level)

    where = jnp.stack([core, x, y]).astype(jnp.int32)
    tables = prep(where, pieces)
    sample = student(noise, tables, pieces)
    is_student = (h == 0) & (parity == 0)
    got = [
        lax.ppermute(sample, ("h", "z"), [(0, 5), (2, 7)]),
        lax.ppermute(sample, ("h", "z"), [(0, 4), (2, 6)]),
        lax.ppermute(sample, ("h", "z"), [(0, 1), (2, 3)]),
    ]
    sample = jnp.where(
        is_student, sample, jnp.where(h == 0, got[2], jnp.where(parity == 1, got[0], got[1]))
    )
    rows, pred, sums, projected, factor, normed = second(
        sample, fresh, level, text, tables, pieces
    )

    real = lax.ppermute(pred, ("h", "z"), [(1, 5), (3, 7)])
    fake = lax.ppermute(pred, ("h", "z"), [(4, 5), (6, 7)])
    total = jnp.zeros((ROWS, CH), f32)
    slopes, pfs = [], []
    rounds = [[("c", CORE)], [("z", Z2)]] + [[(a, shift(4, k)) for k in (1, 2, 3)] for a in "xy"]
    for j, sends in enumerate(rounds):
        sums, rows = lax.optimization_barrier((sums, rows))
        moved = [lax.ppermute(sums, axis, pairs) for axis, pairs in sends]
        total, slope, pf, *small = back_step(
            j, rows, normed, tables, total, pieces[j * 5 : j * 5 + 5]
        )
        ef = small[0] if j == 0 else ef
        pfs.append(pf)
        total, moved = lax.optimization_barrier((total, moved))
        slopes.append(slope)
        sums = sum(moved, sums)
    absolute = lax.ppermute(sums[:8], ("h", "z"), [(1, 5), (3, 7)])
    reward = finish(sums, tables[0], ef, projected, factor, total, slopes, pfs)
    weight = jnp.sum(absolute[:, CH:], axis=1) / (4096.0 * CH)
    weight = 1.0 / (weight + epsilon)
    weight = packed_rows(jnp.broadcast_to(weight[:, None, None], (8, 64, CH)))
    result = weight * (fake - real) - reward
    landed = 0.0
    for to_h in range(2):
        for to_c in range(2):
            pairs = [
                (9 + 4 * c + 2 * q, 8 * to_h + 4 * to_c + 2 * q + c)
                for c in range(2)
                for q in range(2)
            ]
            landed = landed + lax.ppermute(result, NET + ("z",), pairs)
    out = jnp.concatenate([landed[:, :CH], landed[:, CH:]], axis=0)
    return out.reshape(8, 64, CH)


def solution(mesh):
    cube = Mesh(mesh.devices.reshape(2, 2, 4, 4, 4), NET + FSDP)
    placed = (
        P(None, FSDP, None),
        P(None, FSDP, None),
        P(),
        P(),
        P(NET, None, FSDP),
        P(NET, FSDP, None),
        P(NET, FSDP, None),
        P(NET + FSDP, None),
    )
    return jax.shard_map(
        on_device, mesh=cube, in_specs=placed, out_specs=P(None, FSDP, None), check_vma=False
    )
```

```python
import jax
import jax.numpy as jnp
from jax import lax
from jax.experimental import pallas as pl
from jax.experimental.pallas import tpu as pltpu
from jax.sharding import Mesh, PartitionSpec as P

epsilon = 1e-06
NET = ("h", "c")
FSDP = ("z", "x", "y")
ROWS, CH, D, SHARD, PADDED = 512, 64, 2432, 38, 40
PIECE = 4 * PADDED
KDIM = 64 * PADDED
CHUNKS = ((0, 3), (3, 4), (7, 3))
ANY = pl.BlockSpec(memory_space=pl.ANY)
LIMIT_A, LIMIT_B, LIMIT_C = 18, 16, 8
HALF = ROWS // 2
VM = pl.BlockSpec(memory_space=pltpu.VMEM)
SM = pl.BlockSpec(memory_space=pltpu.SMEM)
NT = (((1,), (1,)), ((), ()))
f32, bf16 = jnp.float32, jnp.bfloat16


def call(body, outs, limit, scratch=(), smem=0, ins=0, anys=0):
    return pl.pallas_call(
        body,
        out_shape=[jax.ShapeDtypeStruct(s, t) for s, t in outs],
        in_specs=[SM] * smem + [VM] * ins + [ANY] * anys,
        out_specs=[VM] * len(outs),
        scratch_shapes=list(scratch),
        compiler_params=pltpu.CompilerParams(vmem_limit_bytes=limit * 1024 * 1024),
    )


def fetch(pieces, full, sems):
    copies = [
        pltpu.make_async_copy(ref, full.at[pl.ds(i * PIECE, PIECE), :], sems.at[i])
        for i, ref in enumerate(pieces)
    ]
    for copy in copies:
        copy.start()
    return copies


def mm(a, b):
    return jnp.dot(a, b, preferred_element_type=f32)


def mm_nt(a, b):
    return lax.dot_general(a, b, NT, preferred_element_type=f32)


def unpack(v):
    return jnp.concatenate([v[:, :CH], v[:, CH:]], axis=0)


def pack(v):
    return jnp.concatenate([v[:HALF], v[HALF:]], axis=1)


def order_tails(where_ref, tails, close_ref, en_ref, fin_ref, padded):
    core, x, y = where_ref[0], where_ref[1], where_ref[2]
    for side in range(2):
        parity = core if side == 0 else 1 - core
        for part in range(2):
            z = 2 * part + parity
            for k in range(4):
                at_k = (side * 8 + part * 4 + k) * PIECE
                tail = tails[at_k : at_k + PIECE, :]
                close_ref[at_k : at_k + PIECE, :] = tail[:, :CH]
                tail = tail.astype(f32)
                for i in range(4):
                    xs = i if part == 0 else lax.rem(x + 4 - k, 4)
                    ys = lax.rem(y + 4 - k, 4) if part == 0 else i
                    at = ((z * 4 + xs) * 4 + ys) * PADDED
                    padded[pl.ds(pl.multiple_of(at, 8), PADDED), :] = tail[
                        i * PADDED : (i + 1) * PADDED
                    ]
    for d in range(64):
        padded[d * SHARD : (d + 1) * SHARD, :] = padded[d * PADDED : d * PADDED + SHARD, :]

    def cut(i, _):
        at = pl.multiple_of(i * 128, 128)
        rows = padded[pl.ds(at, 128), :]
        en_ref[pl.ds(at, 128), :] = rows[:, :CH].astype(bf16)
        fin_ref[pl.ds(at, 128), :] = rows[:, CH:].astype(bf16)
        return 0

    lax.fori_loop(0, D // 128, cut, 0)


def forward(rows, close_ref, en_ref, fin_ref, copies, full, active, wide, normed, squares):
    def act(i, _):
        at = pl.multiple_of(i * 256, 256)
        hidden = mm_nt(rows, close_ref[pl.ds(at, 256), :])
        active[:, pl.ds(at, 256)] = jax.nn.gelu(hidden).astype(bf16)
        return 0

    lax.fori_loop(0, KDIM // 256, act, 0)
    squares[...] = jnp.zeros((ROWS, 128), f32)
    for copy in copies:
        copy.wait()

    def tile(at, size):
        for r in range(0, ROWS, HALF):
            total = mm(active[r : r + HALF, :], full[:, pl.ds(at, size)])
            total += mm_nt(rows[r : r + HALF], en_ref[pl.ds(at, size), :])
            wide[r : r + HALF, pl.ds(at, size)] = total
            part = total[:, :128] * total[:, :128]
            for lane in range(128, size, 128):
                part += total[:, lane : lane + 128] * total[:, lane : lane + 128]
            squares[r : r + HALF] += part

    def step(i, _):
        tile(pl.multiple_of(i * 768, 256), 768)
        return 0

    lax.fori_loop(0, 3, step, 0)
    tile(2304, 128)
    mean = jnp.sum(squares[...], axis=1, keepdims=True) / D
    factor = lax.rsqrt(mean + epsilon)
    squares[...] = jnp.broadcast_to(factor, (ROWS, 128))

    def scale(i, _):
        at = pl.multiple_of(i * 128, 128)
        normed[:, pl.ds(at, 128)] = (wide[:, pl.ds(at, 128)] * squares[...]).astype(bf16)
        return 0

    lax.fori_loop(0, D // 128, scale, 0)
    return mm(normed[...], fin_ref[...])


ACTIVE = pltpu.VMEM((ROWS, KDIM), bf16)
WIDE = pltpu.VMEM((ROWS, D), f32)
NORMED = pltpu.VMEM((ROWS, D), bf16)
SQUARES = pltpu.VMEM((ROWS, 128), f32)


SEMS = pltpu.SemaphoreType.DMA((16,))


def student_body(where_ref, rows_ref, *refs):
    pieces, (out_ref, full, close_ref, en_ref, fin_ref) = refs[:16], refs[16:21]
    active, wide, normed, squares, tails, padded, sems, tail_sems = refs[21:]
    small = [
        pltpu.make_async_copy(
            ref.at[:, pl.ds(D, 2 * CH)], tails.at[pl.ds(i * PIECE, PIECE), :], tail_sems.at[i]
        )
        for i, ref in enumerate(pieces)
    ]
    for copy in small:
        copy.start()
    copies = fetch(pieces, full, sems)
    for copy in small:
        copy.wait()
    order_tails(where_ref, tails, close_ref, en_ref, fin_ref, padded)
    rows = unpack(rows_ref[...])
    projected = forward(
        rows, close_ref, en_ref, fin_ref, copies, full, active, wide, normed, squares
    )
    out_ref[...] = pack((rows.astype(f32) + projected)).astype(bf16)


def student(where, rows, pieces):
    out, *tables = call(
        student_body,
        [
            ((HALF, 128), bf16),
            ((KDIM, KDIM), bf16),
            ((KDIM, CH), bf16),
            ((D, CH), bf16),
            ((D, CH), bf16),
        ],
        LIMIT_A,
        [
            ACTIVE,
            WIDE,
            NORMED,
            SQUARES,
            pltpu.VMEM((KDIM, 2 * CH), bf16),
            pltpu.VMEM((KDIM, 2 * CH), f32),
            SEMS,
            SEMS,
        ],
        1,
        1,
        16,
    )(where, rows, *pieces)
    return out, tables


def second_body(sample_ref, renoise_ref, level_ref, text_ref, full, close_ref, en_ref, fin_ref, *refs):
    rows_ref, pred_ref, sums_ref, proj_ref, squares, normed, active, wide = refs
    level = level_ref[...]
    sample = sample_ref[...].astype(f32)
    packed = ((1.0 - level) * sample + level * renoise_ref[...].astype(f32)).astype(bf16)
    rows_ref[...] = packed
    rows = unpack(packed)
    projected = forward(
        rows, close_ref, en_ref, fin_ref, (), full, active, wide, normed, squares
    )
    proj_ref[...] = projected
    judged = rows.astype(f32) + projected
    pred = packed.astype(f32) - level * pack(judged)
    pred_ref[...] = pred
    spread = jnp.abs(sample - pred)
    for p in range(4):
        part = jnp.sum(spread[p * 64 : p * 64 + 64], axis=0, keepdims=True)
        for q, cut in ((p, part[:, :CH]), (p + 4, part[:, CH:])):
            pool = jnp.sum(judged[q * 64 : q * 64 + 64], axis=0, keepdims=True)
            sums_ref[q : q + 1, :] = jnp.concatenate([pool, cut], axis=1)
    sums_ref[8:16, :] = text_ref[...]


def second(sample, renoise, level, text, tables):
    return call(
        second_body,
        [
            ((HALF, 128), bf16),
            ((HALF, 128), f32),
            ((16, 128), f32),
            ((ROWS, CH), f32),
            ((ROWS, 128), f32),
            ((ROWS, D), bf16),
        ],
        LIMIT_B,
        [ACTIVE, WIDE],
        0,
        8,
    )(sample, renoise, level, text, *tables)


def pf_body(full, en_ref, fin_ref, out_ref, ef_ref):
    def tile(i, _):
        at = pl.multiple_of(i * 256, 256)
        out_ref[pl.ds(at, 256), :] = mm(full[pl.ds(at, 256), :D], fin_ref[...])
        return 0

    lax.fori_loop(0, KDIM // 256, tile, 0)
    ef_ref[...] = lax.dot_general(
        en_ref[...], fin_ref[...], (((0,), (0,)), ((), ())), preferred_element_type=f32
    )


def proj_final(full, en, fin):
    return call(pf_body, [((KDIM, CH), f32), ((CH, CH), f32)], LIMIT_C, (), 0, 3)(full, en, fin)


def back_body(base, tiles, rows_ref, normed_ref, full, close_ref, en_ref, sum_ref, *refs):
    out_ref, slope_ref = refs
    rows = unpack(rows_ref[...])
    if base == 0:
        out_ref[...] = mm(normed_ref[...], en_ref[...])
    else:
        out_ref[...] = sum_ref[...]

    def tile(i, _):
        at = pl.multiple_of(base * 256 + i * 256, 256)
        embed = close_ref[pl.ds(at, 256), :]
        hidden = mm_nt(rows, embed)
        s = 0.7978845608028654
        square = hidden * hidden
        th = jnp.tanh(s * hidden * (1.0 + 0.044715 * square))
        slope = 0.5 * (1.0 + th) + (0.5 * s) * hidden * (1.0 - th * th) * (1.0 + 0.134145 * square)
        slope_ref[:, pl.ds(pl.multiple_of(i * 256, 256), 256)] = slope.astype(bf16)
        moved = mm_nt(normed_ref[...], full[pl.ds(at, 256), :D]) * slope
        out_ref[...] += mm(moved.astype(bf16), embed)
        return 0

    lax.fori_loop(0, tiles, tile, 0)


def back_step(chunk, rows, normed, tables, total):
    base, tiles = chunk
    full, close, en, _ = tables
    return call(
        lambda *refs: back_body(base, tiles, *refs),
        [((ROWS, CH), f32), ((ROWS, tiles * 256), bf16)],
        LIMIT_C,
        (),
        0,
        6,
    )(rows, normed, full, close, en, total)


def finish_body(sums_ref, close_ref, pf_ref, ef_ref, proj_ref, factor_ref, total_ref, *refs):
    slopes, (out_ref, carried, result) = refs[:3], refs[3:]
    high = lax.Precision.HIGHEST
    pooled = sums_ref[:8, :CH] / 4096.0
    text = sums_ref[8:16, :CH]
    pooled_norm = jnp.sqrt(jnp.sum(pooled * pooled, axis=-1, keepdims=True) + epsilon)
    text_norm = jnp.sqrt(jnp.sum(text * text, axis=-1, keepdims=True) + epsilon)
    unit_pool = pooled / pooled_norm
    unit_text = text / text_norm
    reward = jnp.sum(unit_pool * unit_text, axis=-1, keepdims=True)
    cot = (unit_text - reward * unit_pool) / pooled_norm
    direct = lax.dot_general(cot, ef_ref[...], NT, precision=high, preferred_element_type=f32)

    def rows_of(v):
        return jnp.concatenate(
            [jnp.broadcast_to(v[p : p + 1], (64, v.shape[1])) for p in range(8)], axis=0
        )

    carried[...] = lax.dot_general(
        cot, pf_ref[...], NT, precision=high, preferred_element_type=f32
    )
    result[...] = rows_of(direct)
    for (base, tiles), ref in zip(CHUNKS, slopes):

        def tile(i, _, base=base, ref=ref):
            at = pl.multiple_of(base * 256 + i * 256, 256)
            local = pl.multiple_of(i * 256, 256)
            scaled = ref[:, pl.ds(local, 256)].astype(f32) * rows_of(carried[:, pl.ds(at, 256)])
            result[...] += mm(scaled.astype(bf16), close_ref[pl.ds(at, 256), :])
            return 0

        lax.fori_loop(0, tiles, tile, 0)
    cot_rows = rows_of(cot)
    along = jnp.sum(cot_rows * proj_ref[...], axis=1, keepdims=True) / D
    out_ref[...] = pack(
        factor_ref[:, :CH] * (result[...] - along * total_ref[...]) + cot_rows
    )


def finish(sums, close, pf, ef, projected, factor, total, slopes):
    return call(
        finish_body,
        [((HALF, 128), f32)],
        LIMIT_C,
        [pltpu.VMEM((8, KDIM), f32), pltpu.VMEM((ROWS, CH), f32)],
        0,
        10,
    )(sums, close, pf, ef, projected, factor, total, *slopes)[0]


def shift(n, k):
    return [(i, (i + k) % n) for i in range(n)]


Z1 = [(0, 1), (1, 0), (2, 3), (3, 2)]
Z2 = [(0, 2), (2, 0), (1, 3), (3, 1)]
CORE = [(0, 1), (1, 0)]


def gather_axis(piece, axis):
    return [piece] + [lax.ppermute(piece, axis, shift(4, k)) for k in range(1, 4)]


def place(me, moved):
    out = jnp.zeros((4,) + moved[0].shape, moved[0].dtype)
    for k, piece in enumerate(moved):
        out = lax.dynamic_update_index_in_dim(out, piece, lax.rem(me - k + 4, 4), 0)
    return out.reshape((4 * moved[0].shape[0],) + moved[0].shape[1:])


def gather_weights(slab, exchange):
    core, z, x, y = (lax.axis_index(a) for a in ("c", "z", "x", "y"))
    swapped = lax.ppermute(slab, ("c", "z"), [(4, 1), (1, 4), (6, 3), (3, 6)])
    mine = jnp.where(core == lax.rem(z, 2), slab, swapped)
    far = lax.ppermute(mine, "z", Z2)
    part_a, part_b = jnp.where(z < 2, mine, far), jnp.where(z < 2, far, mine)
    part_a, part_b = lax.optimization_barrier((part_a, part_b))
    moved_a, moved_b = gather_axis(part_a, "x"), gather_axis(part_b, "y")
    moved_a, moved_b = lax.optimization_barrier((moved_a, moved_b))
    part_a, part_b = lax.optimization_barrier((place(x, moved_a), place(y, moved_b)))
    pieces = gather_axis(part_a, "y") + gather_axis(part_b, "x")
    extra = exchange(part_a)
    first = [0, 4, 1, 5, 3, 7]
    ready, extra = lax.optimization_barrier(([pieces[i] for i in first], extra))
    swaps = {i: lax.ppermute(v, "c", CORE) for i, v in zip(first, ready)}
    pieces = [ready[first.index(i)] if i in first else pieces[i] for i in range(8)]
    for i in (2, 6):
        swaps[i] = lax.ppermute(pieces[i], "c", CORE)
    return pieces + [swaps[i] for i in range(8)], extra


def packed_rows(block):
    flat = block.reshape(ROWS, CH)
    return jnp.concatenate([flat[:HALF], flat[HALF:]], axis=1)


def on_device(noise_in, renoise, timesteps, prompt_ids, embed_w, proj_w, final_w, text_table):
    h, core, z, x, y = (lax.axis_index(a) for a in NET + FSDP)
    parity = lax.rem(z, 2)
    slab = jnp.concatenate([proj_w[0], embed_w[0].T, final_w[0]], axis=1)
    slab = jnp.pad(slab, ((0, PADDED - SHARD), (0, 0)))


    def exchange(anchor):
        _, first, second_in, ids = lax.optimization_barrier(
            (anchor, noise_in, renoise, prompt_ids)
        )
        both = jnp.concatenate([packed_rows(first), packed_rows(second_in)], axis=0)
        other = lax.ppermute(both, "z", Z1)
        table_rows = text_table.shape[0]
        first_row = lax.axis_index(NET + FSDP) * table_rows
        offsets = ids - first_row
        matches = offsets[:, :, None] == jnp.arange(table_rows, dtype=jnp.int32)[None, None, :]
        counts = jnp.sum(matches.astype(f32), axis=1).astype(bf16)
        text = jnp.dot(counts, text_table, preferred_element_type=f32) / ids.shape[1]
        text = jnp.concatenate([text, jnp.zeros_like(text)], axis=1)
        text = text + lax.ppermute(text, "z", Z1)
        text = text + lax.ppermute(text, "h", CORE)
        return jnp.where(core == parity, both, other), text

    pieces, (both, text) = gather_weights(slab, exchange)
    noise, fresh = both[:HALF], both[HALF:]

    judge = (h == 1) & (parity == 1)
    level = timesteps.astype(f32) / 1000.0
    level = jnp.where(judge, 0.0, level)
    level = jnp.broadcast_to(level[:, None, None], (8, 64, CH))
    level = packed_rows(level)

    where = jnp.stack([core, x, y]).astype(jnp.int32)
    sample, tables = student(where, noise, pieces)
    is_student = (h == 0) & (parity == 0)
    got = [
        lax.ppermute(sample, ("h", "z"), [(0, 5), (2, 7)]),
        lax.ppermute(sample, ("h", "z"), [(0, 4), (2, 6)]),
        lax.ppermute(sample, ("h", "z"), [(0, 1), (2, 3)]),
    ]
    full, close, en, fin = tables
    pf, ef = proj_final(full, en, fin)
    got, sample, pf = lax.optimization_barrier((got, sample, pf))
    sample = jnp.where(
        is_student, sample, jnp.where(h == 0, got[2], jnp.where(parity == 1, got[0], got[1]))
    )
    rows, pred, sums, projected, factor, normed = second(
        sample, fresh, level, text, tables
    )

    real = lax.ppermute(pred, ("h", "z"), [(1, 5), (3, 7)])
    fake = lax.ppermute(pred, ("h", "z"), [(4, 5), (6, 7)])
    total = jnp.zeros((ROWS, CH), f32)
    slopes = []
    corners = [("c", CORE), ("z", Z2), (("c", "z"), [(i, i ^ 6) for i in range(8)])]
    rounds = [corners] + [[(a, shift(4, k)) for k in (1, 2, 3)] for a in "xy"]
    for chunk, sends in zip(CHUNKS, rounds):
        sums, rows = lax.optimization_barrier((sums, rows))
        moved = [lax.ppermute(sums, axis, pairs) for axis, pairs in sends]
        total, slope = back_step(chunk, rows, normed, tables, total)
        total, moved = lax.optimization_barrier((total, moved))
        slopes.append(slope)
        sums = sum(moved, sums)
    absolute = lax.ppermute(sums[:8], ("h", "z"), [(1, 5), (3, 7)])
    reward = finish(sums, close, pf, ef, projected, factor, total, slopes)
    weight = jnp.sum(absolute[:, CH:], axis=1) / (4096.0 * CH)
    weight = 1.0 / (weight + epsilon)
    weight = packed_rows(jnp.broadcast_to(weight[:, None, None], (8, 64, CH)))
    result = weight * (fake - real) - reward
    landed = 0.0
    for to_h in range(2):
        for to_c in range(2):
            pairs = [
                (9 + 4 * c + 2 * q, 8 * to_h + 4 * to_c + 2 * q + c)
                for c in range(2)
                for q in range(2)
            ]
            landed = landed + lax.ppermute(result, NET + ("z",), pairs)
    out = jnp.concatenate([landed[:, :CH], landed[:, CH:]], axis=0)
    return out.reshape(8, 64, CH)


def solution(mesh):
    cube = Mesh(mesh.devices.reshape(2, 2, 4, 4, 4), NET + FSDP)
    placed = (
        P(None, FSDP, None),
        P(None, FSDP, None),
        P(),
        P(),
        P(NET, None, FSDP),
        P(NET, FSDP, None),
        P(NET, FSDP, None),
        P(NET + FSDP, None),
    )
    return jax.shard_map(
        on_device, mesh=cube, in_specs=placed, out_specs=P(None, FSDP, None), check_vma=False
    )
```

```python
import jax
import jax.numpy as jnp
from jax import lax
from jax.experimental import pallas as pl
from jax.experimental.pallas import tpu as pltpu
from jax.sharding import Mesh, PartitionSpec as P

epsilon = 1e-06
NET = ("h", "c")
FSDP = ("z", "x", "y")
ROWS, CH, D, SHARD, PADDED = 512, 64, 2432, 38, 40
PIECE = 4 * PADDED
KDIM = 64 * PADDED
CHUNKS = ((0, 3), (3, 4), (7, 3))
ANY = pl.BlockSpec(memory_space=pl.ANY)
LIMIT_A, LIMIT_B, LIMIT_C = 18, 16, 8
HALF = ROWS // 2
VM = pl.BlockSpec(memory_space=pltpu.VMEM)
SM = pl.BlockSpec(memory_space=pltpu.SMEM)
NT = (((1,), (1,)), ((), ()))
f32, bf16 = jnp.float32, jnp.bfloat16


def call(body, outs, limit, scratch=(), smem=0, ins=0, anys=0):
    return pl.pallas_call(
        body,
        out_shape=[jax.ShapeDtypeStruct(s, t) for s, t in outs],
        in_specs=[SM] * smem + [VM] * ins + [ANY] * anys,
        out_specs=[VM] * len(outs),
        scratch_shapes=list(scratch),
        compiler_params=pltpu.CompilerParams(vmem_limit_bytes=limit * 1024 * 1024),
    )


def fetch(pieces, full, sems):
    copies = [
        pltpu.make_async_copy(ref, full.at[pl.ds(i * PIECE, PIECE), :], sems.at[i])
        for i, ref in enumerate(pieces)
    ]
    for copy in copies:
        copy.start()
    return copies


def mm(a, b):
    return jnp.dot(a, b, preferred_element_type=f32)


def mm_nt(a, b):
    return lax.dot_general(a, b, NT, preferred_element_type=f32)


def unpack(v):
    return jnp.concatenate([v[:, :CH], v[:, CH:]], axis=0)


def pack(v):
    return jnp.concatenate([v[:HALF], v[HALF:]], axis=1)


def order_tails(where_ref, tails, close_ref, en_ref, fin_ref, padded):
    core, x, y = where_ref[0], where_ref[1], where_ref[2]
    for side in range(2):
        parity = core if side == 0 else 1 - core
        for part in range(2):
            z = 2 * part + parity
            for k in range(4):
                at_k = (side * 8 + part * 4 + k) * PIECE
                tail = tails[at_k : at_k + PIECE, :]
                close_ref[at_k : at_k + PIECE, :] = tail[:, :CH]
                tail = tail.astype(f32)
                for i in range(4):
                    xs = i if part == 0 else lax.rem(x + 4 - k, 4)
                    ys = lax.rem(y + 4 - k, 4) if part == 0 else i
                    at = ((z * 4 + xs) * 4 + ys) * PADDED
                    padded[pl.ds(pl.multiple_of(at, 8), PADDED), :] = tail[
                        i * PADDED : (i + 1) * PADDED
                    ]
    for d in range(64):
        padded[d * SHARD : (d + 1) * SHARD, :] = padded[d * PADDED : d * PADDED + SHARD, :]

    def cut(i, _):
        at = pl.multiple_of(i * 128, 128)
        rows = padded[pl.ds(at, 128), :]
        en_ref[pl.ds(at, 128), :] = rows[:, :CH].astype(bf16)
        fin_ref[pl.ds(at, 128), :] = rows[:, CH:].astype(bf16)
        return 0

    lax.fori_loop(0, D // 128, cut, 0)


def activate(rows, close_ref, active):
    def act(i, _):
        at = pl.multiple_of(i * 256, 256)
        hidden = mm_nt(rows, close_ref[pl.ds(at, 256), :])
        active[:, pl.ds(at, 256)] = jax.nn.gelu(hidden).astype(bf16)
        return 0

    lax.fori_loop(0, KDIM // 256, act, 0)


def forward(rows, en_ref, fin_ref, full, active, wide, normed, squares):
    squares[...] = jnp.zeros((ROWS, 128), f32)

    def tile(at, size):
        for r in range(0, ROWS, HALF):
            total = mm(active[r : r + HALF, :], full[:, pl.ds(at, size)])
            total += mm_nt(rows[r : r + HALF], en_ref[pl.ds(at, size), :])
            wide[r : r + HALF, pl.ds(at, size)] = total
            part = total[:, :128] * total[:, :128]
            for lane in range(128, size, 128):
                part += total[:, lane : lane + 128] * total[:, lane : lane + 128]
            squares[r : r + HALF] += part

    def step(i, _):
        tile(pl.multiple_of(i * 768, 256), 768)
        return 0

    lax.fori_loop(0, 3, step, 0)
    tile(2304, 128)
    mean = jnp.sum(squares[...], axis=1, keepdims=True) / D
    factor = lax.rsqrt(mean + epsilon)
    squares[...] = jnp.broadcast_to(factor, (ROWS, 128))

    def scale(i, _):
        at = pl.multiple_of(i * 128, 128)
        normed[:, pl.ds(at, 128)] = (wide[:, pl.ds(at, 128)] * squares[...]).astype(bf16)
        return 0

    lax.fori_loop(0, D // 128, scale, 0)
    return mm(normed[...], fin_ref[...])


ACTIVE = pltpu.VMEM((ROWS, KDIM), bf16)
WIDE = pltpu.VMEM((ROWS, D), f32)
NORMED = pltpu.VMEM((ROWS, D), bf16)
SQUARES = pltpu.VMEM((ROWS, 128), f32)


SEMS = pltpu.SemaphoreType.DMA((16,))


def student_body(where_ref, rows_ref, *refs):
    pieces, (out_ref, full, close_ref, en_ref, fin_ref) = refs[:16], refs[16:21]
    active, wide, normed, squares, tails, padded, sems, tail_sems = refs[21:]
    small = [
        pltpu.make_async_copy(
            ref.at[:, pl.ds(D, 2 * CH)], tails.at[pl.ds(i * PIECE, PIECE), :], tail_sems.at[i]
        )
        for i, ref in enumerate(pieces)
    ]
    for copy in small:
        copy.start()
    copies = fetch(pieces, full, sems)
    for copy in small:
        copy.wait()
    order_tails(where_ref, tails, close_ref, en_ref, fin_ref, padded)
    mine = where_ref[3] == 1

    @pl.when(mine)
    def _():
        activate(unpack(rows_ref[...]), close_ref, active)

    for copy in copies:
        copy.wait()

    @pl.when(mine)
    def _():
        rows = unpack(rows_ref[...])
        projected = forward(rows, en_ref, fin_ref, full, active, wide, normed, squares)
        out_ref[...] = pack((rows.astype(f32) + projected)).astype(bf16)

    @pl.when(jnp.logical_not(mine))
    def _():
        out_ref[...] = jnp.zeros((HALF, 128), bf16)


def student(where, rows, pieces):
    out, *tables = call(
        student_body,
        [
            ((HALF, 128), bf16),
            ((KDIM, KDIM), bf16),
            ((KDIM, CH), bf16),
            ((D, CH), bf16),
            ((D, CH), bf16),
        ],
        LIMIT_A,
        [
            ACTIVE,
            WIDE,
            NORMED,
            SQUARES,
            pltpu.VMEM((KDIM, 2 * CH), bf16),
            pltpu.VMEM((KDIM, 2 * CH), f32),
            SEMS,
            SEMS,
        ],
        1,
        1,
        16,
    )(where, rows, *pieces)
    return out, tables


def second_body(sample_ref, renoise_ref, level_ref, text_ref, full, close_ref, en_ref, fin_ref, *refs):
    rows_ref, pred_ref, sums_ref, proj_ref, squares, normed, active, wide = refs
    level = level_ref[...]
    sample = sample_ref[...].astype(f32)
    packed = ((1.0 - level) * sample + level * renoise_ref[...].astype(f32)).astype(bf16)
    rows_ref[...] = packed
    rows = unpack(packed)
    activate(rows, close_ref, active)
    projected = forward(rows, en_ref, fin_ref, full, active, wide, normed, squares)
    proj_ref[...] = projected
    judged = rows.astype(f32) + projected
    pred = packed.astype(f32) - level * pack(judged)
    pred_ref[...] = pred
    spread = jnp.abs(sample - pred)
    for p in range(4):
        part = jnp.sum(spread[p * 64 : p * 64 + 64], axis=0, keepdims=True)
        for q, cut in ((p, part[:, :CH]), (p + 4, part[:, CH:])):
            pool = jnp.sum(judged[q * 64 : q * 64 + 64], axis=0, keepdims=True)
            sums_ref[q : q + 1, :] = jnp.concatenate([pool, cut], axis=1)
    sums_ref[8:16, :] = text_ref[...]


def second(sample, renoise, level, text, tables):
    return call(
        second_body,
        [
            ((HALF, 128), bf16),
            ((HALF, 128), f32),
            ((16, 128), f32),
            ((ROWS, CH), f32),
            ((ROWS, 128), f32),
            ((ROWS, D), bf16),
        ],
        LIMIT_B,
        [ACTIVE, WIDE],
        0,
        8,
    )(sample, renoise, level, text, *tables)


def pf_body(full, en_ref, fin_ref, out_ref, ef_ref):
    def tile(i, _):
        at = pl.multiple_of(i * 256, 256)
        out_ref[pl.ds(at, 256), :] = mm(full[pl.ds(at, 256), :D], fin_ref[...])
        return 0

    lax.fori_loop(0, KDIM // 256, tile, 0)
    ef_ref[...] = lax.dot_general(
        en_ref[...], fin_ref[...], (((0,), (0,)), ((), ())), preferred_element_type=f32
    )


def proj_final(full, en, fin):
    return call(pf_body, [((KDIM, CH), f32), ((CH, CH), f32)], LIMIT_C, (), 0, 3)(full, en, fin)


def back_body(base, tiles, rows_ref, normed_ref, full, close_ref, en_ref, sum_ref, *refs):
    out_ref, slope_ref = refs
    rows = unpack(rows_ref[...])
    if base == 0:
        out_ref[...] = mm(normed_ref[...], en_ref[...])
    else:
        out_ref[...] = sum_ref[...]

    def tile(i, _):
        at = pl.multiple_of(base * 256 + i * 256, 256)
        embed = close_ref[pl.ds(at, 256), :]
        hidden = mm_nt(rows, embed)
        s = 0.7978845608028654
        square = hidden * hidden
        th = jnp.tanh(s * hidden * (1.0 + 0.044715 * square))
        slope = 0.5 * (1.0 + th) + (0.5 * s) * hidden * (1.0 - th * th) * (1.0 + 0.134145 * square)
        slope_ref[:, pl.ds(pl.multiple_of(i * 256, 256), 256)] = slope.astype(bf16)
        moved = mm_nt(normed_ref[...], full[pl.ds(at, 256), :D]) * slope
        out_ref[...] += mm(moved.astype(bf16), embed)
        return 0

    lax.fori_loop(0, tiles, tile, 0)


def back_step(chunk, rows, normed, tables, total):
    base, tiles = chunk
    full, close, en, _ = tables
    return call(
        lambda *refs: back_body(base, tiles, *refs),
        [((ROWS, CH), f32), ((ROWS, tiles * 256), bf16)],
        LIMIT_C,
        (),
        0,
        6,
    )(rows, normed, full, close, en, total)


def finish_body(sums_ref, close_ref, pf_ref, ef_ref, proj_ref, factor_ref, total_ref, *refs):
    slopes, (out_ref, carried, result) = refs[:3], refs[3:]
    high = lax.Precision.HIGHEST
    pooled = sums_ref[:8, :CH] / 4096.0
    text = sums_ref[8:16, :CH]
    pooled_norm = jnp.sqrt(jnp.sum(pooled * pooled, axis=-1, keepdims=True) + epsilon)
    text_norm = jnp.sqrt(jnp.sum(text * text, axis=-1, keepdims=True) + epsilon)
    unit_pool = pooled / pooled_norm
    unit_text = text / text_norm
    reward = jnp.sum(unit_pool * unit_text, axis=-1, keepdims=True)
    cot = (unit_text - reward * unit_pool) / pooled_norm
    direct = lax.dot_general(cot, ef_ref[...], NT, precision=high, preferred_element_type=f32)

    def rows_of(v):
        return jnp.concatenate(
            [jnp.broadcast_to(v[p : p + 1], (64, v.shape[1])) for p in range(8)], axis=0
        )

    carried[...] = lax.dot_general(
        cot, pf_ref[...], NT, precision=high, preferred_element_type=f32
    )
    result[...] = rows_of(direct)
    for (base, tiles), ref in zip(CHUNKS, slopes):

        def tile(i, _, base=base, ref=ref):
            at = pl.multiple_of(base * 256 + i * 256, 256)
            local = pl.multiple_of(i * 256, 256)
            scaled = ref[:, pl.ds(local, 256)].astype(f32) * rows_of(carried[:, pl.ds(at, 256)])
            result[...] += mm(scaled.astype(bf16), close_ref[pl.ds(at, 256), :])
            return 0

        lax.fori_loop(0, tiles, tile, 0)
    cot_rows = rows_of(cot)
    along = jnp.sum(cot_rows * proj_ref[...], axis=1, keepdims=True) / D
    out_ref[...] = pack(
        factor_ref[:, :CH] * (result[...] - along * total_ref[...]) + cot_rows
    )


def finish(sums, close, pf, ef, projected, factor, total, slopes):
    return call(
        finish_body,
        [((HALF, 128), f32)],
        LIMIT_C,
        [pltpu.VMEM((8, KDIM), f32), pltpu.VMEM((ROWS, CH), f32)],
        0,
        10,
    )(sums, close, pf, ef, projected, factor, total, *slopes)[0]


def shift(n, k):
    return [(i, (i + k) % n) for i in range(n)]


Z1 = [(0, 1), (1, 0), (2, 3), (3, 2)]
Z2 = [(0, 2), (2, 0), (1, 3), (3, 1)]
CORE = [(0, 1), (1, 0)]


def gather_axis(piece, axis):
    return [piece] + [lax.ppermute(piece, axis, shift(4, k)) for k in range(1, 4)]


def place(me, moved):
    out = jnp.zeros((4,) + moved[0].shape, moved[0].dtype)
    for k, piece in enumerate(moved):
        out = lax.dynamic_update_index_in_dim(out, piece, lax.rem(me - k + 4, 4), 0)
    return out.reshape((4 * moved[0].shape[0],) + moved[0].shape[1:])


def gather_weights(slab, exchange):
    core, z, x, y = (lax.axis_index(a) for a in ("c", "z", "x", "y"))
    swapped = lax.ppermute(slab, ("c", "z"), [(4, 1), (1, 4), (6, 3), (3, 6)])
    mine = jnp.where(core == lax.rem(z, 2), slab, swapped)
    far = lax.ppermute(mine, "z", Z2)
    part_a, part_b = jnp.where(z < 2, mine, far), jnp.where(z < 2, far, mine)
    part_a, part_b = lax.optimization_barrier((part_a, part_b))
    moved_a, moved_b = gather_axis(part_a, "x"), gather_axis(part_b, "y")
    moved_a, moved_b = lax.optimization_barrier((moved_a, moved_b))
    part_a, part_b = lax.optimization_barrier((place(x, moved_a), place(y, moved_b)))
    pieces = gather_axis(part_a, "y") + gather_axis(part_b, "x")
    extra = exchange(part_a)
    first = [0, 4, 1, 5, 3, 7]
    ready, extra = lax.optimization_barrier(([pieces[i] for i in first], extra))
    swaps = {i: lax.ppermute(v, "c", CORE) for i, v in zip(first, ready)}
    pieces = [ready[first.index(i)] if i in first else pieces[i] for i in range(8)]
    for i in (2, 6):
        swaps[i] = lax.ppermute(pieces[i], "c", CORE)
    return pieces + [swaps[i] for i in range(8)], extra


def packed_rows(block):
    flat = block.reshape(ROWS, CH)
    return jnp.concatenate([flat[:HALF], flat[HALF:]], axis=1)


def on_device(noise_in, renoise, timesteps, prompt_ids, embed_w, proj_w, final_w, text_table):
    h, core, z, x, y = (lax.axis_index(a) for a in NET + FSDP)
    parity = lax.rem(z, 2)
    slab = jnp.concatenate([proj_w[0], embed_w[0].T, final_w[0]], axis=1)
    slab = jnp.pad(slab, ((0, PADDED - SHARD), (0, 0)))


    def exchange(anchor):
        _, first, second_in, ids = lax.optimization_barrier(
            (anchor, noise_in, renoise, prompt_ids)
        )
        both = jnp.concatenate([packed_rows(first), packed_rows(second_in)], axis=0)
        other = lax.ppermute(both, "z", Z1)
        table_rows = text_table.shape[0]
        first_row = lax.axis_index(NET + FSDP) * table_rows
        offsets = ids - first_row
        matches = offsets[:, :, None] == jnp.arange(table_rows, dtype=jnp.int32)[None, None, :]
        counts = jnp.sum(matches.astype(f32), axis=1).astype(bf16)
        text = jnp.dot(counts, text_table, preferred_element_type=f32) / ids.shape[1]
        text = jnp.concatenate([text, jnp.zeros_like(text)], axis=1)
        text = text + lax.ppermute(text, "z", Z1)
        text = text + lax.ppermute(text, "h", CORE)
        return jnp.where(core == parity, both, other), text

    pieces, (both, text) = gather_weights(slab, exchange)
    noise, fresh = both[:HALF], both[HALF:]

    judge = (h == 1) & (parity == 1)
    level = timesteps.astype(f32) / 1000.0
    level = jnp.where(judge, 0.0, level)
    level = jnp.broadcast_to(level[:, None, None], (8, 64, CH))
    level = packed_rows(level)

    is_student = (h == 0) & (parity == 0)
    where = jnp.stack([core, x, y, is_student.astype(jnp.int32)]).astype(jnp.int32)
    sample, tables = student(where, noise, pieces)
    got = [
        lax.ppermute(sample, ("h", "z"), [(0, 5), (2, 7)]),
        lax.ppermute(sample, ("h", "z"), [(0, 4), (2, 6)]),
        lax.ppermute(sample, ("h", "z"), [(0, 1), (2, 3)]),
    ]
    full, close, en, fin = tables
    pf, ef = proj_final(full, en, fin)
    got, sample, pf = lax.optimization_barrier((got, sample, pf))
    sample = jnp.where(
        is_student, sample, jnp.where(h == 0, got[2], jnp.where(parity == 1, got[0], got[1]))
    )
    rows, pred, sums, projected, factor, normed = second(
        sample, fresh, level, text, tables
    )

    real = lax.ppermute(pred, ("h", "z"), [(1, 5), (3, 7)])
    fake = lax.ppermute(pred, ("h", "z"), [(4, 5), (6, 7)])
    total = jnp.zeros((ROWS, CH), f32)
    slopes = []
    corners = [("c", CORE), ("z", Z2), (("c", "z"), [(i, i ^ 6) for i in range(8)])]
    rounds = [corners] + [[(a, shift(4, k)) for k in (1, 2, 3)] for a in "xy"]
    for chunk, sends in zip(CHUNKS, rounds):
        sums, rows = lax.optimization_barrier((sums, rows))
        moved = [lax.ppermute(sums, axis, pairs) for axis, pairs in sends]
        total, slope = back_step(chunk, rows, normed, tables, total)
        total, moved = lax.optimization_barrier((total, moved))
        slopes.append(slope)
        sums = sum(moved, sums)
    absolute = lax.ppermute(sums[:8], ("h", "z"), [(1, 5), (3, 7)])
    reward = finish(sums, close, pf, ef, projected, factor, total, slopes)
    weight = jnp.sum(absolute[:, CH:], axis=1) / (4096.0 * CH)
    weight = 1.0 / (weight + epsilon)
    weight = packed_rows(jnp.broadcast_to(weight[:, None, None], (8, 64, CH)))
    result = weight * (fake - real) - reward
    landed = 0.0
    for to_h in range(2):
        for to_c in range(2):
            pairs = [
                (9 + 4 * c + 2 * q, 8 * to_h + 4 * to_c + 2 * q + c)
                for c in range(2)
                for q in range(2)
            ]
            landed = landed + lax.ppermute(result, NET + ("z",), pairs)
    out = jnp.concatenate([landed[:, :CH], landed[:, CH:]], axis=0)
    return out.reshape(8, 64, CH)


def solution(mesh):
    cube = Mesh(mesh.devices.reshape(2, 2, 4, 4, 4), NET + FSDP)
    placed = (
        P(None, FSDP, None),
        P(None, FSDP, None),
        P(),
        P(),
        P(NET, None, FSDP),
        P(NET, FSDP, None),
        P(NET, FSDP, None),
        P(NET + FSDP, None),
    )
    return jax.shard_map(
        on_device, mesh=cube, in_specs=placed, out_specs=P(None, FSDP, None), check_vma=False
    )
```

```python
import jax
import jax.numpy as jnp
from jax import lax
from jax.experimental import pallas as pl
from jax.experimental.pallas import tpu as pltpu
from jax.sharding import Mesh, PartitionSpec as P

epsilon = 1e-06
NET = ("h", "c")
FSDP = ("z", "x", "y")
ROWS, CH, D, SHARD, PADDED = 512, 64, 2432, 38, 40
PIECE = 4 * PADDED
KDIM = 64 * PADDED
CHUNKS = ((0, 3), (3, 4), (7, 3))
ANY = pl.BlockSpec(memory_space=pl.ANY)
LIMIT_A, LIMIT_B, LIMIT_C = 18, 16, 8
HALF = ROWS // 2
VM = pl.BlockSpec(memory_space=pltpu.VMEM)
SM = pl.BlockSpec(memory_space=pltpu.SMEM)
NT = (((1,), (1,)), ((), ()))
f32, bf16 = jnp.float32, jnp.bfloat16


def call(body, outs, limit, scratch=(), smem=0, ins=0, anys=0):
    return pl.pallas_call(
        body,
        out_shape=[jax.ShapeDtypeStruct(s, t) for s, t in outs],
        in_specs=[SM] * smem + [VM] * ins + [ANY] * anys,
        out_specs=[VM] * len(outs),
        scratch_shapes=list(scratch),
        compiler_params=pltpu.CompilerParams(vmem_limit_bytes=limit * 1024 * 1024),
    )


def fetch(pieces, full, sems):
    copies = [
        pltpu.make_async_copy(ref, full.at[pl.ds(i * PIECE, PIECE), :], sems.at[i])
        for i, ref in enumerate(pieces)
    ]
    for copy in copies:
        copy.start()
    return copies


def mm(a, b):
    return jnp.dot(a, b, preferred_element_type=f32)


def mm_nt(a, b):
    return lax.dot_general(a, b, NT, preferred_element_type=f32)


def unpack(v):
    return jnp.concatenate([v[:, :CH], v[:, CH:]], axis=0)


def pack(v):
    return jnp.concatenate([v[:HALF], v[HALF:]], axis=1)


def order_tails(where_ref, tails, close_ref, en_ref, fin_ref, padded):
    core, x, y = where_ref[0], where_ref[1], where_ref[2]
    for side in range(2):
        parity = core if side == 0 else 1 - core
        for part in range(2):
            z = 2 * part + parity
            for k in range(4):
                at_k = (side * 8 + part * 4 + k) * PIECE
                tail = tails[at_k : at_k + PIECE, :]
                close_ref[at_k : at_k + PIECE, :] = tail[:, :CH]
                tail = tail.astype(f32)
                for i in range(4):
                    xs = i if part == 0 else lax.rem(x + 4 - k, 4)
                    ys = lax.rem(y + 4 - k, 4) if part == 0 else i
                    at = ((z * 4 + xs) * 4 + ys) * PADDED
                    padded[pl.ds(pl.multiple_of(at, 8), PADDED), :] = tail[
                        i * PADDED : (i + 1) * PADDED
                    ]
    for d in range(64):
        padded[d * SHARD : (d + 1) * SHARD, :] = padded[d * PADDED : d * PADDED + SHARD, :]

    def cut(i, _):
        at = pl.multiple_of(i * 128, 128)
        rows = padded[pl.ds(at, 128), :]
        en_ref[pl.ds(at, 128), :] = rows[:, :CH].astype(bf16)
        fin_ref[pl.ds(at, 128), :] = rows[:, CH:].astype(bf16)
        return 0

    lax.fori_loop(0, D // 128, cut, 0)


def activate(rows, close_ref, active):
    def act(i, _):
        at = pl.multiple_of(i * 256, 256)
        hidden = mm_nt(rows, close_ref[pl.ds(at, 256), :])
        active[:, pl.ds(at, 256)] = jax.nn.gelu(hidden).astype(bf16)
        return 0

    lax.fori_loop(0, KDIM // 256, act, 0)


def forward(rows, en_ref, fin_ref, full, active, wide, normed, squares):
    squares[...] = jnp.zeros((ROWS, 128), f32)

    def tile(at, size):
        for r in range(0, ROWS, HALF):
            total = mm(active[r : r + HALF, :], full[:, pl.ds(at, size)])
            total += mm_nt(rows[r : r + HALF], en_ref[pl.ds(at, size), :])
            wide[r : r + HALF, pl.ds(at, size)] = total
            part = total[:, :128] * total[:, :128]
            for lane in range(128, size, 128):
                part += total[:, lane : lane + 128] * total[:, lane : lane + 128]
            squares[r : r + HALF] += part

    def step(i, _):
        tile(pl.multiple_of(i * 768, 256), 768)
        return 0

    lax.fori_loop(0, 3, step, 0)
    tile(2304, 128)
    mean = jnp.sum(squares[...], axis=1, keepdims=True) / D
    factor = lax.rsqrt(mean + epsilon)
    squares[...] = jnp.broadcast_to(factor, (ROWS, 128))

    def scale(i, _):
        at = pl.multiple_of(i * 128, 128)
        normed[:, pl.ds(at, 128)] = (wide[:, pl.ds(at, 128)] * squares[...]).astype(bf16)
        return 0

    lax.fori_loop(0, D // 128, scale, 0)
    return mm(normed[...], fin_ref[...])


ACTIVE = pltpu.VMEM((ROWS, KDIM), bf16)
WIDE = pltpu.VMEM((ROWS, D), f32)
NORMED = pltpu.VMEM((ROWS, D), bf16)
SQUARES = pltpu.VMEM((ROWS, 128), f32)


SEMS = pltpu.SemaphoreType.DMA((16,))


def student_body(where_ref, rows_ref, *refs):
    pieces, (out_ref, full, close_ref, en_ref, fin_ref) = refs[:16], refs[16:21]
    active, wide, normed, squares, tails, padded, sems, tail_sems = refs[21:]
    small = [
        pltpu.make_async_copy(
            ref.at[:, pl.ds(D, 2 * CH)], tails.at[pl.ds(i * PIECE, PIECE), :], tail_sems.at[i]
        )
        for i, ref in enumerate(pieces)
    ]
    for copy in small:
        copy.start()
    copies = fetch(pieces, full, sems)
    for copy in small:
        copy.wait()
    order_tails(where_ref, tails, close_ref, en_ref, fin_ref, padded)
    mine = where_ref[3] == 1

    @pl.when(mine)
    def _():
        activate(unpack(rows_ref[...]), close_ref, active)

    for copy in copies:
        copy.wait()

    @pl.when(mine)
    def _():
        rows = unpack(rows_ref[...])
        projected = forward(rows, en_ref, fin_ref, full, active, wide, normed, squares)
        out_ref[...] = pack((rows.astype(f32) + projected)).astype(bf16)

    @pl.when(jnp.logical_not(mine))
    def _():
        out_ref[...] = jnp.zeros((HALF, 128), bf16)


def student(where, rows, pieces):
    out, *tables = call(
        student_body,
        [
            ((HALF, 128), bf16),
            ((KDIM, KDIM), bf16),
            ((KDIM, CH), bf16),
            ((D, CH), bf16),
            ((D, CH), bf16),
        ],
        LIMIT_A,
        [
            ACTIVE,
            WIDE,
            NORMED,
            SQUARES,
            pltpu.VMEM((KDIM, 2 * CH), bf16),
            pltpu.VMEM((KDIM, 2 * CH), f32),
            SEMS,
            SEMS,
        ],
        1,
        1,
        16,
    )(where, rows, *pieces)
    return out, tables


def second_body(sample_ref, renoise_ref, level_ref, text_ref, full, close_ref, en_ref, fin_ref, *refs):
    rows_ref, pred_ref, sums_ref, proj_ref, squares, normed, active, wide = refs
    level = level_ref[...]
    sample = sample_ref[...].astype(f32)
    packed = ((1.0 - level) * sample + level * renoise_ref[...].astype(f32)).astype(bf16)
    rows_ref[...] = packed
    rows = unpack(packed)
    activate(rows, close_ref, active)
    projected = forward(rows, en_ref, fin_ref, full, active, wide, normed, squares)
    proj_ref[...] = projected
    judged = rows.astype(f32) + projected
    pred = packed.astype(f32) - level * pack(judged)
    pred_ref[...] = pred
    spread = jnp.abs(sample - pred)
    for p in range(4):
        part = jnp.sum(spread[p * 64 : p * 64 + 64], axis=0, keepdims=True)
        for q, cut in ((p, part[:, :CH]), (p + 4, part[:, CH:])):
            pool = jnp.sum(judged[q * 64 : q * 64 + 64], axis=0, keepdims=True)
            sums_ref[q : q + 1, :] = jnp.concatenate([pool, cut], axis=1)
    sums_ref[8:16, :] = text_ref[...]


def second(sample, renoise, level, text, tables):
    return call(
        second_body,
        [
            ((HALF, 128), bf16),
            ((HALF, 128), f32),
            ((16, 128), f32),
            ((ROWS, CH), f32),
            ((ROWS, 128), f32),
            ((ROWS, D), bf16),
        ],
        LIMIT_B,
        [ACTIVE, WIDE],
        0,
        8,
    )(sample, renoise, level, text, *tables)


def pf_body(full, en_ref, fin_ref, out_ref, ef_ref):
    def tile(i, _):
        at = pl.multiple_of(i * 256, 256)
        out_ref[pl.ds(at, 256), :] = mm(full[pl.ds(at, 256), :D], fin_ref[...])
        return 0

    lax.fori_loop(0, KDIM // 256, tile, 0)
    ef_ref[...] = lax.dot_general(
        en_ref[...], fin_ref[...], (((0,), (0,)), ((), ())), preferred_element_type=f32
    )


def proj_final(full, en, fin):
    return call(pf_body, [((KDIM, CH), f32), ((CH, CH), f32)], LIMIT_C, (), 0, 3)(full, en, fin)


def back_body(base, tiles, rows_ref, normed_ref, full, close_ref, en_ref, sum_ref, *refs):
    out_ref, slope_ref = refs
    rows = unpack(rows_ref[...])
    if base == 0:
        out_ref[...] = mm(normed_ref[...], en_ref[...])
    else:
        out_ref[...] = sum_ref[...]

    def tile(i, _):
        at = pl.multiple_of(base * 256 + i * 256, 256)
        embed = close_ref[pl.ds(at, 256), :]
        hidden = mm_nt(rows, embed)
        s = 0.7978845608028654
        square = hidden * hidden
        th = jnp.tanh(s * hidden * (1.0 + 0.044715 * square))
        slope = 0.5 * (1.0 + th) + (0.5 * s) * hidden * (1.0 - th * th) * (1.0 + 0.134145 * square)
        slope_ref[:, pl.ds(pl.multiple_of(i * 256, 256), 256)] = slope.astype(bf16)
        moved = mm_nt(normed_ref[...], full[pl.ds(at, 256), :D]) * slope
        out_ref[...] += mm(moved.astype(bf16), embed)
        return 0

    lax.fori_loop(0, tiles, tile, 0)


def back_step(chunk, rows, normed, tables, total):
    base, tiles = chunk
    full, close, en, _ = tables
    return call(
        lambda *refs: back_body(base, tiles, *refs),
        [((ROWS, CH), f32), ((ROWS, tiles * 256), bf16)],
        LIMIT_C,
        (),
        0,
        6,
    )(rows, normed, full, close, en, total)


def finish_body(sums_ref, close_ref, pf_ref, ef_ref, proj_ref, factor_ref, total_ref, *refs):
    slopes, (out_ref, carried, result) = refs[:3], refs[3:]
    high = lax.Precision.HIGHEST
    pooled = sums_ref[:8, :CH] / 4096.0
    text = sums_ref[8:16, :CH]
    pooled_norm = jnp.sqrt(jnp.sum(pooled * pooled, axis=-1, keepdims=True) + epsilon)
    text_norm = jnp.sqrt(jnp.sum(text * text, axis=-1, keepdims=True) + epsilon)
    unit_pool = pooled / pooled_norm
    unit_text = text / text_norm
    reward = jnp.sum(unit_pool * unit_text, axis=-1, keepdims=True)
    cot = (unit_text - reward * unit_pool) / pooled_norm
    direct = lax.dot_general(cot, ef_ref[...], NT, precision=high, preferred_element_type=f32)

    def rows_of(v):
        return jnp.concatenate(
            [jnp.broadcast_to(v[p : p + 1], (64, v.shape[1])) for p in range(8)], axis=0
        )

    carried[...] = lax.dot_general(
        cot, pf_ref[...], NT, precision=high, preferred_element_type=f32
    )
    result[...] = rows_of(direct)
    for (base, tiles), ref in zip(CHUNKS, slopes):

        def tile(i, _, base=base, ref=ref):
            at = pl.multiple_of(base * 256 + i * 256, 256)
            local = pl.multiple_of(i * 256, 256)
            scaled = ref[:, pl.ds(local, 256)].astype(f32) * rows_of(carried[:, pl.ds(at, 256)])
            result[...] += mm(scaled.astype(bf16), close_ref[pl.ds(at, 256), :])
            return 0

        lax.fori_loop(0, tiles, tile, 0)
    cot_rows = rows_of(cot)
    along = jnp.sum(cot_rows * proj_ref[...], axis=1, keepdims=True) / D
    out_ref[...] = pack(
        factor_ref[:, :CH] * (result[...] - along * total_ref[...]) + cot_rows
    )


def finish(sums, close, pf, ef, projected, factor, total, slopes):
    return call(
        finish_body,
        [((HALF, 128), f32)],
        LIMIT_C,
        [pltpu.VMEM((8, KDIM), f32), pltpu.VMEM((ROWS, CH), f32)],
        0,
        10,
    )(sums, close, pf, ef, projected, factor, total, *slopes)[0]


def shift(n, k):
    return [(i, (i + k) % n) for i in range(n)]


Z1 = [(0, 1), (1, 0), (2, 3), (3, 2)]
Z2 = [(0, 2), (2, 0), (1, 3), (3, 1)]
CORE = [(0, 1), (1, 0)]


def gather_axis(piece, axis):
    return [piece] + [lax.ppermute(piece, axis, shift(4, k)) for k in range(1, 4)]


def place(me, moved):
    out = jnp.zeros((4,) + moved[0].shape, moved[0].dtype)
    for k, piece in enumerate(moved):
        out = lax.dynamic_update_index_in_dim(out, piece, lax.rem(me - k + 4, 4), 0)
    return out.reshape((4 * moved[0].shape[0],) + moved[0].shape[1:])


def gather_weights(slab, exchange):
    core, z, x, y = (lax.axis_index(a) for a in ("c", "z", "x", "y"))
    swapped = lax.ppermute(slab, ("c", "z"), [(4, 1), (1, 4), (6, 3), (3, 6)])
    mine = jnp.where(core == lax.rem(z, 2), slab, swapped)
    far = lax.ppermute(mine, "z", Z2)
    part_a, part_b = jnp.where(z < 2, mine, far), jnp.where(z < 2, far, mine)
    part_a, part_b = lax.optimization_barrier((part_a, part_b))
    moved_a, moved_b = gather_axis(part_a, "x"), gather_axis(part_b, "y")
    moved_a, moved_b = lax.optimization_barrier((moved_a, moved_b))
    part_a, part_b = lax.optimization_barrier((place(x, moved_a), place(y, moved_b)))
    pieces = gather_axis(part_a, "y") + gather_axis(part_b, "x")
    extra = exchange(part_a)
    first = [0, 4, 1, 5, 3, 7]
    ready, extra = lax.optimization_barrier(([pieces[i] for i in first], extra))
    swaps = {i: lax.ppermute(v, "c", CORE) for i, v in zip(first, ready)}
    pieces = [ready[first.index(i)] if i in first else pieces[i] for i in range(8)]
    for i in (2, 6):
        swaps[i] = lax.ppermute(pieces[i], "c", CORE)
    return pieces + [swaps[i] for i in range(8)], extra


def packed_rows(block):
    flat = block.reshape(ROWS, CH)
    return jnp.concatenate([flat[:HALF], flat[HALF:]], axis=1)


def on_device(noise_in, renoise, timesteps, prompt_ids, embed_w, proj_w, final_w, text_table):
    h, core, z, x, y = (lax.axis_index(a) for a in NET + FSDP)
    parity = lax.rem(z, 2)
    slab = jnp.concatenate([proj_w[0], embed_w[0].T, final_w[0]], axis=1)
    slab = jnp.pad(slab, ((0, PADDED - SHARD), (0, 0)))


    def exchange(anchor):
        _, first, second_in, ids = lax.optimization_barrier(
            (anchor, noise_in, renoise, prompt_ids)
        )
        both = jnp.concatenate([packed_rows(first), packed_rows(second_in)], axis=0)
        other = lax.ppermute(both, ("c", "z"), [(5, 4), (7, 6), (0, 1), (2, 3)])
        table_rows = text_table.shape[0]
        first_row = lax.axis_index(NET + FSDP) * table_rows
        offsets = ids - first_row
        matches = offsets[:, :, None] == jnp.arange(table_rows, dtype=jnp.int32)[None, None, :]
        counts = jnp.sum(matches.astype(f32), axis=1).astype(bf16)
        text = jnp.dot(counts, text_table, preferred_element_type=f32) / ids.shape[1]
        text = jnp.concatenate([text, jnp.zeros_like(text)], axis=1)
        text = text + lax.ppermute(text, "z", Z1)
        text = text + lax.ppermute(text, "h", CORE)
        return jnp.where(core == parity, both, other), text

    pieces, (both, text) = gather_weights(slab, exchange)
    noise, fresh = both[:HALF], both[HALF:]

    judge = (h == 1) & (parity == 1)
    level = timesteps.astype(f32) / 1000.0
    level = jnp.where(judge, 0.0, level)
    level = jnp.broadcast_to(level[:, None, None], (8, 64, CH))
    level = packed_rows(level)

    is_student = (h == 0) & (parity == 0)
    where = jnp.stack([core, x, y, is_student.astype(jnp.int32)]).astype(jnp.int32)
    sample, tables = student(where, noise, pieces)
    got = [
        lax.ppermute(sample, ("h", "z"), [(0, 5), (2, 7)]),
        lax.ppermute(sample, ("h", "z"), [(0, 4), (2, 6)]),
        lax.ppermute(sample, ("h", "z"), [(0, 1), (2, 3)]),
    ]
    full, close, en, fin = tables
    pf, ef = proj_final(full, en, fin)
    got, sample, pf = lax.optimization_barrier((got, sample, pf))
    sample = jnp.where(
        is_student, sample, jnp.where(h == 0, got[2], jnp.where(parity == 1, got[0], got[1]))
    )
    rows, pred, sums, projected, factor, normed = second(
        sample, fresh, level, text, tables
    )

    real = lax.ppermute(pred, ("h", "z"), [(1, 5), (3, 7)])
    fake = lax.ppermute(pred, ("h", "z"), [(4, 5), (6, 7)])
    total = jnp.zeros((ROWS, CH), f32)
    slopes = []
    corners = [("c", CORE), ("z", Z2), (("c", "z"), [(i, i ^ 6) for i in range(8)])]
    rounds = [corners] + [[(a, shift(4, k)) for k in (1, 2, 3)] for a in "xy"]
    for chunk, sends in zip(CHUNKS, rounds):
        sums, rows = lax.optimization_barrier((sums, rows))
        moved = [lax.ppermute(sums, axis, pairs) for axis, pairs in sends]
        total, slope = back_step(chunk, rows, normed, tables, total)
        total, moved = lax.optimization_barrier((total, moved))
        slopes.append(slope)
        sums = sum(moved, sums)
    absolute = lax.ppermute(sums[:8], ("h", "z"), [(1, 5), (3, 7)])
    reward = finish(sums, close, pf, ef, projected, factor, total, slopes)
    weight = jnp.sum(absolute[:, CH:], axis=1) / (4096.0 * CH)
    weight = 1.0 / (weight + epsilon)
    weight = packed_rows(jnp.broadcast_to(weight[:, None, None], (8, 64, CH)))
    result = weight * (fake - real) - reward
    landed = 0.0
    for to_h in range(2):
        for to_c in range(2):
            pairs = [
                (9 + 4 * c + 2 * q, 8 * to_h + 4 * to_c + 2 * q + c)
                for c in range(2)
                for q in range(2)
            ]
            landed = landed + lax.ppermute(result, NET + ("z",), pairs)
    out = jnp.concatenate([landed[:, :CH], landed[:, CH:]], axis=0)
    return out.reshape(8, 64, CH)


def solution(mesh):
    cube = Mesh(mesh.devices.reshape(2, 2, 4, 4, 4), NET + FSDP)
    placed = (
        P(None, FSDP, None),
        P(None, FSDP, None),
        P(),
        P(),
        P(NET, None, FSDP),
        P(NET, FSDP, None),
        P(NET, FSDP, None),
        P(NET + FSDP, None),
    )
    return jax.shard_map(
        on_device, mesh=cube, in_specs=placed, out_specs=P(None, FSDP, None), check_vma=False
    )
```
